256 devices in a mesh: row: 32 (over x, z), col: 8 (over y, core).
Axes of the slice: x: 4, y: 4, z: 8, core: 2. Of those that a mesh axis runs over, the one named last changes fastest.
Arguments:
- features: bfloat16 [524288, 128], P(('row', 'col')), may hold values from -6 to 6
- w_self: bfloat16 [128, 256], replicated, may hold values from -0.5 to 0.5
- w_neigh: bfloat16 [128, 256], replicated, may hold values from -2 to 2
- bias: float32 [256], replicated, may hold values from -3 to 3
- cotangent: bfloat16 [524288, 256], P(('row', 'col')), may hold values from -6 to 6
- local_tiles: bfloat16 [16384, 128, 128], P(('row', 'col')), may hold values from 0 to 1, as said below
- local_tile_idx: int32 [16384, 2], P(('row', 'col')), may hold values from 0 to 15, as said below
- boundary_adj: bfloat16 [524288, 1024], P(('row', 'col')), may hold values from 0 to 1, as said below
- send_rows: int32 [2048, 128], P(('row', 'col')), may hold values from 0 to 2047
- send_counts: int32 [2048], P(('row', 'col')), may hold values from 96 to 128, as said below
- hub_adj: bfloat16 [524288, 1024], P(('row', 'col')), may hold values from 0 to 1, as said below
- hub_rows: int32 [256, 32], P(('row', 'col')), may hold values from 0 to 2047
Outputs:
- grad_features: bfloat16 [524288, 128], P(('row', 'col'))
- grad_self: float32 [128, 256], replicated
- grad_neigh: float32 [128, 256], replicated
- grad_bias: float32 [256], replicated
The draws below stay inside these ranges and needn't reach their ends.
Inputs may be any that keep to these rules, and one draw needn't show every extreme that they name: `local_tile_idx`: each block's 64 pairs are distinct tile positions of its grid of (16) x (16) tiles. `send_counts`: every block uses all 128 slots of one of its send lists. `send_rows`: entries of unused slots are arbitrary rows; a node may appear in several slots. `hub_rows`: A node may be listed more than once. `boundary_adj`: nonnegative edge weights; columns of unused slots are zero. `hub_adj`: nonnegative edge weights. `local_tiles`: nonnegative edge weights.
All inputs are finite; a program needn't handle non-finite values.
Results may differ from the reference program's by a relative error of at most 0.0075.
Values may be sent and summed in bfloat16 or wider, within the bound.
No kernel may reach another device: no remote copies, remote signals or barrier semaphores. Data moves between devices by JAX's collectives and lax.ppermute only.
A program may use at most 64 MiB of HBM per device.

```python
import math
import jax
import jax.numpy as jnp
from jax import lax

F = 128
H = 256
NODE_DEV = 2048
TILE = 128
SEND_MAX = 128
HUB_DEV = 32
LT = 64
HUBS = 1024
NODES = 524288
N_ROW = 32
N_COL = 8


def sparse_weights(key, shape, density):
    keep_key, value_key = jax.random.split(key)
    keep = jax.random.uniform(keep_key, shape) < density
    values = jnp.exp(jax.random.uniform(value_key, shape, minval=math.log(0.1), maxval=0.0))
    return jnp.where(keep, values, 0.0)


def shared_counts(key):
    base_key, full_key = jax.random.split(key)
    blocks_all = N_ROW * N_COL
    base = jax.random.randint(base_key, (blocks_all, N_COL), max(1, 3 * SEND_MAX // 4), SEND_MAX + 1)
    full_peer = jax.random.randint(full_key, (blocks_all, 1), 0, N_COL)
    counts = jnp.where(jnp.arange(N_COL)[None, :] == full_peer, SEND_MAX, base)
    return counts.reshape(-1).astype(jnp.int32)


def draw_send_counts(key, part):
    return shared_counts(key)


def draw_boundary_adj(key, part):
    counts = shared_counts(key)
    key = jax.random.fold_in(key, 5)
    blocks_all = N_ROW * N_COL
    grid = counts.reshape(N_ROW, N_COL, N_COL)
    limit = jnp.transpose(grid, (0, 2, 1)).reshape(blocks_all, N_COL)
    slot_ok = jnp.arange(SEND_MAX)[None, None, :] < limit[:, :, None]
    slot_ok = slot_ok.reshape(blocks_all, 1, N_COL * SEND_MAX)
    density = min(1.0, 16.0 / (N_COL * SEND_MAX))
    values = sparse_weights(key, (blocks_all, NODE_DEV, N_COL * SEND_MAX), density)
    values = jnp.where(slot_ok, values, 0.0)
    return values.reshape(blocks_all * NODE_DEV, N_COL * SEND_MAX).astype(jnp.bfloat16)


def draw_hub_adj(key, part):
    key = jax.random.fold_in(key, 13)
    density = min(1.0, 8.0 / HUBS)
    return sparse_weights(key, (N_ROW * N_COL * NODE_DEV, HUBS), density).astype(jnp.bfloat16)


def draw_local_tiles(key, part):
    key = jax.random.fold_in(key, 11)
    density = min(1.0, 32.0 / NODE_DEV)
    return sparse_weights(key, (N_ROW * N_COL * LT, TILE, TILE), density).astype(jnp.bfloat16)


def draw_local_tile_idx(key, part):
    key = jax.random.fold_in(key, 9)
    block_count = NODE_DEV // TILE
    keys = jax.random.split(key, N_ROW * N_COL)
    chosen = jax.vmap(lambda one_key: jax.random.permutation(one_key, block_count * block_count)[:LT])(keys)
    pairs = jnp.stack([chosen // block_count, chosen % block_count], axis=-1)
    return pairs.reshape(-1, 2).astype(jnp.int32)


def plant(array, rng, smallest, largest):
    extent = array.shape
    spot = [jax.random.randint(jax.random.fold_in(rng, axis), (), 0, extent[axis]) for axis in range(len(extent))]
    array = array.at[tuple(spot)].set(smallest)
    longest = extent.index(max(extent))
    spot[longest] = (spot[longest] + 1) % extent[longest]
    return array.at[tuple(spot)].set(largest)


def steps_of(rng, extent, pieces, least, largest):
    level, own = 1.0, jax.random.fold_in(rng, 6)
    for axis_at, shards_of in pieces:
        heights = jnp.exp(jax.random.uniform(jax.random.fold_in(own, axis_at), (shards_of,), jnp.float32, least / len(pieces), largest / len(pieces)))
        level = level * jnp.repeat(heights, extent[axis_at] // shards_of).reshape([-1 if axis == axis_at else 1 for axis in range(len(extent))])
    return level


def centred(own_key, dims, deviation, most, pieces=(), kind=jnp.bfloat16):
    entries = deviation * jax.random.normal(own_key, dims, jnp.float32)
    if pieces:
        entries = entries * steps_of(own_key, dims, pieces, -0.22, 0.18)
    return jnp.clip(entries, -most, most).astype(kind)


def setup_inputs(seed: int = 0) -> dict:
    key_list = jax.random.split(jax.random.key(seed), 13)
    features = centred(key_list[0], (NODES, F), 1.0, 6.0, ((0, 256),))
    w_self = centred(key_list[1], (F, H), F ** -0.5, 0.5)
    w_neigh = centred(key_list[2], (F, H), (F // 16) ** -0.5, 2.0)
    bias = centred(key_list[3], (H,), 0.5, 3.0, (), jnp.float32)
    cotangent = centred(key_list[4], (NODES, H), 1.0, 6.0, ((0, 256),))
    local_tiles = draw_local_tiles(jax.random.fold_in(key_list[12], 71), 0)
    local_tile_idx = draw_local_tile_idx(jax.random.fold_in(key_list[12], 71), 0)
    boundary_adj = draw_boundary_adj(jax.random.fold_in(key_list[12], 71), 0)
    send_rows = plant(jax.random.randint(key_list[8], (N_ROW * N_COL * N_COL, SEND_MAX), 0, NODE_DEV), jax.random.fold_in(key_list[8], 1), 0, NODE_DEV - 1).astype(jnp.int32)
    send_counts = draw_send_counts(jax.random.fold_in(key_list[12], 71), 0)
    hub_adj = draw_hub_adj(jax.random.fold_in(key_list[12], 71), 0)
    hub_rows = plant(jax.random.randint(key_list[11], (N_ROW * N_COL, HUB_DEV), 0, NODE_DEV), jax.random.fold_in(key_list[11], 1), 0, NODE_DEV - 1).astype(jnp.int32)
    return dict(features=features, w_self=w_self, w_neigh=w_neigh, bias=bias, cotangent=cotangent, local_tiles=local_tiles, local_tile_idx=local_tile_idx, boundary_adj=boundary_adj, send_rows=send_rows, send_counts=send_counts, hub_adj=hub_adj, hub_rows=hub_rows)


def device_pass(node_rows, tiles, tile_index, bound_adj, received, hub_block, hub_table, cotangent, w_self, w_neigh, bias):
    block_count = NODE_DEV // TILE
    high = lax.Precision.HIGHEST
    row_onehot = (tile_index[:, 0][None, :] == jnp.arange(block_count, dtype=jnp.int32)[:, None]).astype(jnp.float32)
    col_onehot = (tile_index[:, 1][None, :] == jnp.arange(block_count, dtype=jnp.int32)[:, None]).astype(jnp.float32)
    tiles_wide = tiles.astype(jnp.float32)
    gathered = node_rows.reshape(block_count, TILE, F)[tile_index[:, 1]].astype(jnp.float32)
    tile_terms = jnp.einsum('tik,tkf->tif', tiles_wide, gathered, precision=high)
    local_sum = jnp.einsum('bt,tif->bif', row_onehot, tile_terms, precision=high).reshape(NODE_DEV, F)
    tile_degree = jnp.einsum('bt,ti->bi', row_onehot, lax.optimization_barrier(jnp.sum(tiles, axis=2, dtype=jnp.float32)), precision=high).reshape(NODE_DEV)
    boundary_part = jnp.dot(bound_adj, received, preferred_element_type=jnp.float32)
    hub_part = jnp.dot(hub_block, hub_table, preferred_element_type=jnp.float32)
    degree = tile_degree + lax.optimization_barrier(jnp.sum(bound_adj, axis=1, dtype=jnp.float32)) + lax.optimization_barrier(jnp.sum(hub_block, axis=1, dtype=jnp.float32))
    inverse_degree = 1.0 / (1.0 + degree)
    mean_part = ((local_sum + boundary_part + hub_part) * inverse_degree[:, None]).astype(jnp.bfloat16)
    preact = jnp.dot(node_rows, w_self, preferred_element_type=jnp.float32) + jnp.dot(mean_part, w_neigh, preferred_element_type=jnp.float32) + bias
    slope = jnp.where(preact > 0, 1.0, jnp.exp(jnp.minimum(preact, 0.0)))
    preact_grad = (cotangent.astype(jnp.float32) * slope).astype(jnp.bfloat16)
    part_self = jnp.dot(node_rows.T, preact_grad, preferred_element_type=jnp.float32)
    part_neigh = jnp.dot(mean_part.T, preact_grad, preferred_element_type=jnp.float32)
    part_bias = lax.optimization_barrier(jnp.sum(preact_grad, axis=0, dtype=jnp.float32))
    mean_grad = (jnp.dot(preact_grad, w_neigh.T, preferred_element_type=jnp.float32) * inverse_degree[:, None]).astype(jnp.bfloat16)
    grad_blocks = mean_grad.reshape(block_count, TILE, F)[tile_index[:, 0]].astype(jnp.float32)
    tile_back = jnp.einsum('tij,tif->tjf', tiles_wide, grad_blocks, precision=high)
    local_back = jnp.einsum('bt,tjf->bjf', col_onehot, tile_back, precision=high).reshape(NODE_DEV, F)
    local_grad = jnp.dot(preact_grad, w_self.T, preferred_element_type=jnp.float32) + local_back
    boundary_back = jnp.dot(bound_adj.T, mean_grad, preferred_element_type=jnp.float32).astype(jnp.bfloat16)
    hub_back = jnp.dot(hub_block.T, mean_grad, preferred_element_type=jnp.float32)
    return (local_grad, boundary_back, hub_back, part_self, part_neigh, part_bias)

def pick_rows(block_x, picks):
    return block_x[picks]

def reference(features, w_self, w_neigh, bias, cotangent, local_tiles, local_tile_idx, boundary_adj, send_rows, send_counts, hub_adj, hub_rows):
    devices_all = N_ROW * N_COL
    by_block = features.reshape(N_ROW, N_COL, NODE_DEV, F)
    lists = send_rows.reshape(N_ROW, N_COL, N_COL, SEND_MAX)
    used = jnp.arange(SEND_MAX, dtype=jnp.int32)[None, None, None, :] < send_counts.reshape(N_ROW, N_COL, N_COL)[..., None]
    sent = jax.vmap(jax.vmap(pick_rows))(by_block, lists)
    sent = jnp.where(used[..., None], sent, jnp.zeros((), sent.dtype))
    received = jnp.transpose(sent, (0, 2, 1, 3, 4)).reshape(devices_all, N_COL * SEND_MAX, F)
    hub_lists = hub_rows.reshape(N_ROW, N_COL, HUB_DEV)
    hub_x = jax.vmap(jax.vmap(pick_rows))(by_block, hub_lists)
    hub_tables = jnp.transpose(hub_x, (1, 0, 2, 3)).reshape(N_COL, HUBS, F)
    hub_stack = hub_tables[jnp.arange(devices_all, dtype=jnp.int32) % N_COL]
    packed = (features.reshape(devices_all, NODE_DEV, F), local_tiles.reshape(devices_all, LT, TILE, TILE), local_tile_idx.reshape(devices_all, LT, 2), boundary_adj.reshape(devices_all, NODE_DEV, N_COL * SEND_MAX), received, hub_adj.reshape(devices_all, NODE_DEV, HUBS), hub_stack, cotangent.reshape(devices_all, NODE_DEV, H))
    local_grad, boundary_back, hub_back, part_self, part_neigh, part_bias = lax.map(lambda item: device_pass(*item, w_self, w_neigh, bias), packed)
    returned = jnp.transpose(boundary_back.reshape(N_ROW, N_COL, N_COL, SEND_MAX, F), (0, 2, 1, 3, 4))
    returned = jnp.where(used[..., None], returned.astype(jnp.float32), 0.0)
    starts = jnp.arange(devices_all, dtype=jnp.int32).reshape(N_ROW, N_COL) * NODE_DEV
    target = starts[:, :, None, None] + lists
    grad_flat = local_grad.reshape(NODES, F).at[target.reshape(-1)].add(returned.reshape(-1, F))
    hub_sum = lax.optimization_barrier(jnp.sum(hub_back.reshape(N_ROW, N_COL, HUBS, F), axis=0))
    hub_sum = jnp.transpose(hub_sum.reshape(N_COL, N_ROW, HUB_DEV, F), (1, 0, 2, 3))
    hub_target = starts[:, :, None] + hub_lists
    grad_flat = grad_flat.at[hub_target.reshape(-1)].add(hub_sum.reshape(-1, F))
    factor = 1.0 / math.sqrt(NODES)
    return (grad_flat.astype(jnp.bfloat16), lax.optimization_barrier(jnp.sum(part_self, axis=0)) * factor, lax.optimization_barrier(jnp.sum(part_neigh, axis=0)) * factor, lax.optimization_barrier(jnp.sum(part_bias, axis=0)) * factor)
```

```python
import math

import jax
import jax.numpy as jnp
from jax import lax
from jax.sharding import PartitionSpec as P


def block_onehot(block_ids, block_count):
    return (block_ids[None, :] == jnp.arange(block_count, dtype=jnp.int32)[:, None]).astype(
        jnp.float32
    )


def swap(parts, axis):
    return lax.all_to_all(parts, axis, split_axis=0, concat_axis=0, tiled=True)


def body(
    features,
    w_self,
    w_neigh,
    bias,
    cotangent,
    local_tiles,
    local_tile_idx,
    boundary_adj,
    send_rows,
    send_counts,
    hub_adj,
    hub_rows,
):
    high = lax.Precision.HIGHEST
    node_count = features.shape[0]
    feature_width = features.shape[1]
    tile_size = local_tiles.shape[1]
    block_count = node_count // tile_size
    send_max = send_rows.shape[1]
    hub_count = hub_rows.shape[1]
    own_hubs = jnp.take(features, hub_rows[0], axis=0)
    rows = lax.axis_size("row")
    cols = lax.axis_size("col")
    hub_table = swap(
        jnp.broadcast_to(own_hubs[None], (rows, hub_count, feature_width)).reshape(-1, feature_width),
        "row",
    )
    slot_valid = jnp.arange(send_max, dtype=jnp.int32)[None, :] < send_counts[:, None]
    outgoing = jnp.where(slot_valid[:, :, None], features[send_rows], jnp.zeros((), features.dtype))
    received = lax.all_to_all(
        outgoing.reshape(-1, feature_width), "col", split_axis=0, concat_axis=0, tiled=True
    )
    row_onehot = block_onehot(local_tile_idx[:, 0], block_count)
    col_onehot = block_onehot(local_tile_idx[:, 1], block_count)
    gathered = features.reshape(block_count, tile_size, feature_width)[local_tile_idx[:, 1]]
    tile_terms = jnp.einsum(
        "tik,tkf->tif", local_tiles, gathered, preferred_element_type=jnp.float32
    )
    local_sum = jnp.einsum("bt,tif->bif", row_onehot, tile_terms, precision=high).reshape(
        node_count, feature_width
    )
    tile_degree = jnp.einsum(
        "bt,ti->bi", row_onehot, jnp.sum(local_tiles, axis=2, dtype=jnp.float32), precision=high
    ).reshape(node_count)
    boundary_part = jnp.dot(boundary_adj, received, preferred_element_type=jnp.float32)
    hub_part = jnp.dot(hub_adj, hub_table, preferred_element_type=jnp.float32)
    degree = (
        tile_degree
        + jnp.sum(boundary_adj, axis=1, dtype=jnp.float32)
        + jnp.sum(hub_adj, axis=1, dtype=jnp.float32)
    )
    inverse_degree = 1.0 / (1.0 + degree)
    mean_part = ((local_sum + boundary_part + hub_part) * inverse_degree[:, None]).astype(
        jnp.bfloat16
    )
    preact = (
        jnp.dot(features, w_self, preferred_element_type=jnp.float32)
        + jnp.dot(mean_part, w_neigh, preferred_element_type=jnp.float32)
        + bias
    )
    slope = jnp.where(preact > 0, 1.0, jnp.exp(jnp.minimum(preact, 0.0)))
    preact_grad = (cotangent.astype(jnp.float32) * slope).astype(jnp.bfloat16)
    mean_grad = (
        jnp.dot(preact_grad, w_neigh.T, preferred_element_type=jnp.float32)
        * inverse_degree[:, None]
    ).astype(jnp.bfloat16)
    boundary_back = jnp.dot(boundary_adj.T, mean_grad, preferred_element_type=jnp.float32).astype(
        jnp.bfloat16
    )
    hub_back = jnp.dot(hub_adj.T, mean_grad, preferred_element_type=jnp.float32)
    grad_self = jnp.dot(features.T, preact_grad, preferred_element_type=jnp.float32)
    grad_neigh = jnp.dot(mean_part.T, preact_grad, preferred_element_type=jnp.float32)
    grad_bias = jnp.sum(preact_grad, axis=0, dtype=jnp.float32)
    share = grad_self.size // (rows * feature_width)
    first = jnp.concatenate(
        [
            hub_back.reshape(rows, hub_count, feature_width),
            grad_self.reshape(rows, share, feature_width),
            grad_neigh.reshape(rows, share, feature_width),
        ],
        axis=1,
    ).astype(jnp.bfloat16)
    depth = first.shape[1]
    first = swap(first.reshape(-1, feature_width), "row").reshape(rows, depth, feature_width)
    row_sum = jnp.sum(first, axis=0, dtype=jnp.float32)
    hub_mine = row_sum[:hub_count]
    extra = jnp.concatenate(
        [row_sum[hub_count:], grad_bias.reshape(-1, feature_width)], axis=0
    ).astype(jnp.bfloat16)
    pad = -extra.shape[0] % 16
    extra = jnp.pad(extra, ((0, pad), (0, 0)))
    second = jnp.concatenate(
        [
            boundary_back.reshape(cols, send_max, feature_width),
            jnp.broadcast_to(extra[None], (cols,) + extra.shape),
        ],
        axis=1,
    )
    depth = second.shape[1]
    second = swap(second.reshape(-1, feature_width), "col").reshape(cols, depth, feature_width)
    returned = second[:, :send_max].reshape(-1, feature_width)
    col_sum = jnp.sum(second[:, send_max:], axis=0, dtype=jnp.float32)
    third = swap(
        jnp.broadcast_to(col_sum[None], (rows,) + col_sum.shape).reshape(-1, feature_width), "row"
    ).reshape(rows, -1, feature_width)
    width = grad_self.shape[1]
    summed = (
        third[:, :share].reshape(-1, width),
        third[:, share : 2 * share].reshape(-1, width),
        jnp.sum(third[:, 2 * share : 2 * share + width // feature_width], axis=0).reshape(-1),
    )
    grad_blocks = mean_grad.reshape(block_count, tile_size, feature_width)[local_tile_idx[:, 0]]
    tile_back = jnp.einsum(
        "tij,tif->tjf", local_tiles, grad_blocks, preferred_element_type=jnp.float32
    )
    local_back = jnp.einsum("bt,tjf->bjf", col_onehot, tile_back, precision=high).reshape(
        node_count, feature_width
    )
    grad_rows = jnp.dot(preact_grad, w_self.T, preferred_element_type=jnp.float32) + local_back
    returned_wide = jnp.where(slot_valid.reshape(-1)[:, None], returned.astype(jnp.float32), 0.0)
    grad_rows = grad_rows.at[send_rows.reshape(-1)].add(returned_wide)
    grad_rows = grad_rows.at[hub_rows[0]].add(hub_mine)
    total_nodes = node_count * rows * cols
    factor = 1.0 / math.sqrt(total_nodes)
    return (
        grad_rows.astype(jnp.bfloat16),
        summed[0] * factor,
        summed[1] * factor,
        summed[2] * factor,
    )


def solution(mesh):
    placed = (
        P(("row", "col"), None),
        P(),
        P(),
        P(),
        P(("row", "col"), None),
        P(("row", "col"), None, None),
        P(("row", "col"), None),
        P(("row", "col"), None),
        P(("row", "col"), None),
        P(("row", "col")),
        P(("row", "col"), None),
        P(("row", "col"), None),
    )
    return jax.shard_map(
        body,
        mesh=mesh,
        in_specs=placed,
        out_specs=(P(("row", "col"), None), P(), P(), P()),
        check_vma=False,
    )
```

```python
import math

import jax
import jax.numpy as jnp
from jax import lax
from jax.experimental import pallas as pl
from jax.experimental.pallas import tpu as pltpu
from jax.sharding import PartitionSpec as P

BF = jnp.bfloat16
F32 = jnp.float32
LANES = 128
MIB = 1 << 20


def mm(left, right):
    return jnp.dot(left, right, preferred_element_type=F32)


def with_ones(rows):
    return jnp.concatenate([rows, jnp.ones((rows.shape[0], LANES), BF)], axis=1)


def column(row):
    n = row.shape[1]
    down = lax.broadcasted_iota(jnp.int32, (n, n), 0)
    across = lax.broadcasted_iota(jnp.int32, (n, n), 1)
    picked = jnp.where(down == across, row.astype(F32), 0.0)
    return jnp.sum(picked, axis=1, keepdims=True).astype(jnp.int32)


def onehot(match):
    return jnp.where(match, 1.0, 0.0).astype(BF)


def call(kernel, name, out, flops, nbytes, vmem=24, **rest):
    return pl.pallas_call(
        kernel,
        out_shape=out,
        name=name,
        cost_estimate=pl.CostEstimate(flops=flops, bytes_accessed=nbytes, transcendentals=0),
        compiler_params=pltpu.CompilerParams(vmem_limit_bytes=vmem * MIB),
        **rest,
    )


def whole(shape):
    return pl.BlockSpec(shape, lambda *_: (0,) * len(shape))


HBM = pl.BlockSpec(memory_space=pltpu.HBM)
VMEM = pl.BlockSpec(memory_space=pltpu.VMEM)


def fetch(source, target, sem):
    copy = pltpu.make_async_copy(source, target, sem)
    copy.start()
    return copy


def chunks(ref, buf, sems, first):
    size = buf.shape[1]
    return [
        fetch(ref.at[pl.ds(i * size, size)], buf.at[i], sems.at[first + i])
        for i in range(buf.shape[0])
    ]


def hub_rows_kernel(rows_hbm, feat_hbm, out_ref, rows_ref, feat_ref, sems):
    listed = fetch(rows_hbm, rows_ref, sems.at[0])
    feat = fetch(feat_hbm, feat_ref, sems.at[1])
    listed.wait()
    nodes = feat_ref.shape[0]
    lanes = lax.broadcasted_iota(jnp.int32, (rows_ref.shape[1], nodes), 1)
    pick = onehot(lanes == column(rows_ref[...]))
    feat.wait()
    own = mm(pick, feat_ref[...]).astype(BF)
    out_ref[...] = jnp.broadcast_to(own[None], out_ref.shape)


def send_kernel(counts_hbm, rows_hbm, feat_hbm, out_ref, counts_ref, rows_ref, feat_ref, sems):
    counts = fetch(counts_hbm, counts_ref, sems.at[0])
    listed_rows = fetch(rows_hbm, rows_ref, sems.at[1])
    feat = fetch(feat_hbm, feat_ref, sems.at[2])
    counts.wait()
    listed_rows.wait()
    feat.wait()
    nodes = feat_ref.shape[0]
    peers, slots = rows_ref.shape
    lanes = lax.broadcasted_iota(jnp.int32, (slots, nodes), 1)
    slot = lax.broadcasted_iota(jnp.int32, (1, slots), 1)
    for peer in range(peers):
        listed = jnp.where(slot < counts_ref[peer], rows_ref[peer : peer + 1, :], -1)
        out_ref[peer] = mm(onehot(lanes == column(listed)), feat_ref[...]).astype(BF)


def forward_kernel(
    idx_hbm,
    feat_hbm,
    tiles_hbm,
    table_hbm,
    adj_hbm,
    ext_hbm,
    idx_ref,
    feat_ref,
    tiles_ref,
    table_ref,
    adj_ref,
    acc,
    sems,
    out_sems,
):
    index = fetch(idx_hbm, idx_ref, sems.at[0])
    feat = fetch(feat_hbm, feat_ref, sems.at[1])
    tile_parts = chunks(tiles_hbm, tiles_ref, sems, 3)
    table = fetch(table_hbm, table_ref, sems.at[2])
    steps, block, _ = adj_ref.shape
    tile_steps, count, side, _ = tiles_ref.shape
    adj_parts = chunks(adj_hbm, adj_ref, sems, 3 + tile_steps)
    acc[...] = jnp.zeros_like(acc)
    index.wait()
    feat.wait()
    for step in range(tile_steps):
        tile_parts[step].wait()
        for t in range(count):
            k = step * count + t
            to = pl.multiple_of(idx_ref[0, k] * side, side)
            at = pl.multiple_of(idx_ref[1, k] * side, side)
            rows = with_ones(feat_ref[pl.ds(at, side), :])
            acc[pl.ds(to, side), :] += mm(tiles_ref[step, t], rows)
    table.wait()
    hub_table = with_ones(table_ref[...])
    stores = []
    for i in range(steps):
        rows = pl.ds(i * block, block)
        adj_parts[i].wait()
        acc[rows, :] += mm(adj_ref[i], hub_table)
        stores.append(fetch(acc.at[rows], ext_hbm.at[rows], out_sems.at[i]))
    for store in stores:
        store.wait()


def middle_kernel(
    w_self_hbm,
    w_neigh_hbm,
    bias_hbm,
    bound_hbm,
    hub_hbm,
    feat_hbm,
    cot_hbm,
    ext_hbm,
    received_hbm,
    grad_t_hbm,
    pg_hbm,
    first_hbm,
    bias_sum_hbm,
    w_self_ref,
    w_neigh_ref,
    bias_ref,
    bound_ref,
    hub_ref,
    feat_ref,
    cot_ref,
    ext_ref,
    received_ref,
    grad_t_ref,
    pg_ref,
    first_ref,
    bias_sum,
    hub_acc,
    w_acc,
    sems,
    out_sems,
):
    steps, block, width = feat_ref.shape
    small = [
        fetch(received_hbm, received_ref, sems.at[3]),
        fetch(w_self_hbm, w_self_ref, sems.at[0]),
        fetch(w_neigh_hbm, w_neigh_ref, sems.at[1]),
        fetch(bias_hbm, bias_ref, sems.at[2]),
    ]
    pairs = (
        (bound_hbm, bound_ref),
        (ext_hbm, ext_ref),
        (feat_hbm, feat_ref),
        (cot_hbm, cot_ref),
        (hub_hbm, hub_ref),
    )
    large = []
    for i in range(steps):
        rows = pl.ds(i * block, block)
        large.append(
            [
                fetch(source.at[rows], target.at[i], sems.at[4 + 5 * i + j])
                for j, (source, target) in enumerate(pairs)
            ]
        )
    for copy in small:
        copy.wait()
    received = with_ones(received_ref[...])
    w_both = jnp.concatenate([w_self_ref[...], w_neigh_ref[...]], axis=0)
    stores = []
    done = None
    for i in range(steps + 1):
        if i < steps:
            for copy in large[i][:4]:
                copy.wait()
        if i > 0:
            large[i - 1][4].wait()
        if i < steps:
            rows = pl.ds(i * block, block)
            ext = ext_ref[i] + mm(bound_ref[i], received)
            inverse = 1.0 / (1.0 + ext[:, width:])
            mean = (ext[:, :width] * inverse).astype(BF)
            both = jnp.concatenate([feat_ref[i], mean], axis=1)
            preact = mm(both, w_both) + bias_ref[...]
            slope = jnp.where(preact > 0, 1.0, jnp.exp(jnp.minimum(preact, 0.0)))
            pg = (cot_ref[i].astype(F32) * slope).astype(BF)
            pg_ref[i] = pg
            grad = lax.dot_general(
                pg, w_neigh_ref[...], (((1,), (1,)), ((), ())), preferred_element_type=F32
            )
            grad_t = jnp.transpose(grad * inverse).astype(BF)
            grad_t_ref[:, rows] = grad_t
        if i > 0:
            last_both, last_pg, last_grad_t = done
            hub_part = mm(last_grad_t, hub_ref[i - 1])
            w_part = mm(jnp.transpose(last_both), last_pg)
            bias_part = jnp.sum(last_pg.astype(F32), axis=0, keepdims=True)
            if i == 1:
                hub_acc[...] = hub_part
                w_acc[...] = w_part
                bias_sum[...] = bias_part
            else:
                hub_acc[...] += hub_part
                w_acc[...] += w_part
                bias_sum[...] += bias_part
        if i < steps:
            done = (both, pg, grad_t)
            stores.append(fetch(pg_ref.at[i], pg_hbm.at[rows], out_sems.at[2 * i]))
            stores.append(
                fetch(grad_t_ref.at[:, rows], grad_t_hbm.at[:, rows], out_sems.at[2 * i + 1])
            )
    rows, depth, _ = first_ref.shape
    hubs = hub_acc.shape[1] // rows
    share = w_acc.shape[0] // rows
    hub_back = jnp.transpose(hub_acc[...]).astype(BF)
    first_ref[:, :hubs, :] = hub_back.reshape(rows, hubs, width)
    left = w_acc[:, :LANES].reshape(rows, share, LANES)
    right = w_acc[:, LANES:].reshape(rows, share, LANES)
    first_ref[:, hubs:, :] = jnp.concatenate([left, right], axis=1).astype(BF)
    stores.append(fetch(first_ref, first_hbm, out_sems.at[2 * steps]))
    stores.append(fetch(bias_sum, bias_sum_hbm, out_sems.at[2 * steps + 1]))
    for store in stores:
        store.wait()


def boundary_back_kernel(bound_hbm, grad_t_ref, out_ref, bound_ref, acc, sems):
    parts = chunks(bound_hbm, bound_ref, sems, 0)
    steps, block, _ = bound_ref.shape
    for i in range(steps):
        parts[i].wait()
        part = mm(grad_t_ref[:, pl.ds(i * block, block)], bound_ref[i])
        if i == 0:
            acc[...] = part
        else:
            acc[...] += part
    out_ref[...] = jnp.transpose(acc[...]).astype(BF).reshape(out_ref.shape)


def local_back_kernel(
    idx_hbm,
    w_self_hbm,
    tiles_hbm,
    grad_t_ref,
    pg_ref,
    out_ref,
    idx_ref,
    w_self_ref,
    tiles_ref,
    acc,
    sems,
):
    index = fetch(idx_hbm, idx_ref, sems.at[0])
    weights = fetch(w_self_hbm, w_self_ref, sems.at[1])
    parts = chunks(tiles_hbm, tiles_ref, sems, 2)
    acc[...] = jnp.zeros_like(acc)
    steps, count, side, _ = tiles_ref.shape
    index.wait()
    weights.wait()
    for step in range(steps):
        parts[step].wait()
        for t in range(count):
            k = step * count + t
            at = pl.multiple_of(idx_ref[0, k] * side, side)
            acc[idx_ref[1, k]] += mm(grad_t_ref[:, pl.ds(at, side)], tiles_ref[step, t])
    for b in range(acc.shape[0]):
        rows = pl.ds(b * side, side)
        own = lax.dot_general(
            pg_ref[rows, :],
            w_self_ref[...],
            (((1,), (1,)), ((), ())),
            preferred_element_type=F32,
        )
        out_ref[rows, :] = own + jnp.transpose(acc[b])


def split(value):
    high = value.astype(BF)
    return high, (value - high.astype(F32)).astype(BF)


def row_sum_kernel(first_ref, back_ref, bias_ref, hub_ref, second_ref):
    rows, depth, width = first_ref.shape
    total = first_ref[0].astype(F32)
    for r in range(1, rows):
        total += first_ref[r].astype(F32)
    hubs = depth - 16
    hub = total[:hubs]
    high, rest = split(hub)
    middle, low = split(hub - high.astype(F32))
    hub_ref[...] = jnp.concatenate([high, middle, low, jnp.zeros((hubs, width), BF)], axis=0)
    peers, _, _ = second_ref.shape
    slots = back_ref.shape[1]
    w_high, w_low = split(total[hubs:])
    bias = jnp.concatenate([bias_ref[:, :width], bias_ref[:, width:]], axis=0)
    b_rest = bias - bias.astype(BF).astype(F32)
    b_rows = jnp.concatenate([bias, b_rest, jnp.zeros((12, width), F32)], axis=0).astype(BF)
    for p in range(peers):
        second_ref[p, :slots] = back_ref[p]
        second_ref[p, slots : slots + 16] = w_high
        second_ref[p, slots + 16 : slots + 32] = w_low
        second_ref[p, slots + 32 : slots + 48] = b_rows


def col_sum_kernel(second_ref, third_ref):
    peers, depth, width = second_ref.shape
    start = depth - 48
    total = second_ref[0, start:].astype(F32)
    for p in range(1, peers):
        total += second_ref[p, start:].astype(F32)
    weights = total[:16] + total[16:32]
    bias = total[32:34] + total[34:36]
    done = jnp.concatenate([weights, bias, jnp.zeros((6, width), F32)], axis=0)
    third_ref[...] = jnp.broadcast_to(done[None], third_ref.shape)


def scatter_kernel(idx_ref, second_ref, hub_ref, base_ref, out_ref):
    block = out_ref.shape[0]
    peers = second_ref.shape[0]
    slots = idx_ref.shape[1]
    node = lax.broadcasted_iota(jnp.int32, (block, slots), 0) + pl.program_id(0) * block
    match = [onehot(node == idx_ref[p : p + 1, :]) for p in range(peers + 1)]
    values = [second_ref[p, :slots, :] for p in range(peers)] + [hub_ref[...]]
    added = mm(jnp.concatenate(match, axis=1), jnp.concatenate(values, axis=0))
    out_ref[...] = (base_ref[...] + added).astype(BF)


def finish_kernel(third_ref, self_ref, neigh_ref, bias_ref, *, factor):
    rows = third_ref.shape[0]
    share = 8
    left = third_ref[:, :share, :].reshape(rows * share, LANES)
    right = third_ref[:, share : 2 * share, :].reshape(rows * share, LANES)
    grads = jnp.concatenate([left, right], axis=1) * factor
    half = grads.shape[0] // 2
    self_ref[...] = grads[:half]
    neigh_ref[...] = grads[half:]
    bias = third_ref[0, 16:24, :]
    for r in range(1, rows):
        bias += third_ref[r, 16:24, :]
    bias_ref[...] = jnp.concatenate([bias[0:1], bias[1:2]], axis=1) * factor


def swap(parts, axis):
    return lax.all_to_all(parts, axis, split_axis=0, concat_axis=0, tiled=True)


def body(
    features,
    w_self,
    w_neigh,
    bias,
    cotangent,
    local_tiles,
    local_tile_idx,
    boundary_adj,
    send_rows,
    send_counts,
    hub_adj,
    hub_rows,
):
    nodes, width = features.shape
    hidden = w_self.shape[1]
    tiles, side, _ = local_tiles.shape
    peers, slots = send_rows.shape
    hub_own = hub_rows.shape[1]
    rows = lax.axis_size("row")
    cols = lax.axis_size("col")
    hubs = rows * hub_own
    received_rows = peers * slots
    struct = jax.ShapeDtypeStruct
    block = 512
    steps = nodes // block
    tile_steps = 4
    tile_block = tiles // tile_steps

    tile_index = local_tile_idx.T
    sems = lambda count: pltpu.SemaphoreType.DMA((count,))
    int32 = jnp.int32

    hub_send = call(
        hub_rows_kernel,
        "hub_rows",
        struct((rows, hub_own, width), BF),
        2 * hub_own * nodes * width,
        nodes * width * 2,
        vmem=60,
        in_specs=[HBM, HBM],
        scratch_shapes=[
            pltpu.VMEM((1, hub_own), int32),
            pltpu.VMEM((nodes, width), BF),
            sems(2),
        ],
    )(hub_rows, features)
    table = swap(hub_send, "row").reshape(hubs, width)

    outgoing = call(
        send_kernel,
        "send_rows",
        struct((peers, slots, width), BF),
        2 * peers * slots * nodes * width,
        nodes * width * 2,
        vmem=60,
        in_specs=[HBM, HBM, HBM],
        scratch_shapes=[
            pltpu.SMEM((peers,), int32),
            pltpu.VMEM((peers, slots), int32),
            pltpu.VMEM((nodes, width), BF),
            sems(3),
        ],
    )(send_counts, send_rows, features)
    received = swap(outgoing, "col").reshape(received_rows, width)

    ext = call(
        forward_kernel,
        "forward",
        struct((nodes, 2 * width), F32),
        4 * tiles * side * side * width + 4 * nodes * hubs * width,
        tiles * side * side * 2 + nodes * width * 10 + nodes * hubs * 2,
        vmem=60,
        in_specs=[HBM] * 5,
        out_specs=HBM,
        scratch_shapes=[
            pltpu.SMEM((2, tiles), int32),
            pltpu.VMEM((nodes, width), BF),
            pltpu.VMEM((tile_steps, tile_block, side, side), BF),
            pltpu.VMEM((hubs, width), BF),
            pltpu.VMEM((steps, block, hubs), BF),
            pltpu.VMEM((nodes, 2 * width), F32),
            sems(3 + tile_steps + steps),
            sems(steps),
        ],
    )(tile_index, features, local_tiles, table, hub_adj)

    share = 2 * width // rows
    depth = hub_own + 2 * share
    grad_t, pg, first, bias_sum = call(
        middle_kernel,
        "middle",
        (
            struct((width, nodes), BF),
            struct((nodes, hidden), BF),
            struct((rows, depth, width), BF),
            struct((1, hidden), F32),
        ),
        8 * nodes * hubs * width,
        nodes * (hubs * 4 + width * 16),
        vmem=60,
        in_specs=[HBM] * 9,
        out_specs=(HBM,) * 4,
        scratch_shapes=[
            pltpu.VMEM((width, hidden), BF),
            pltpu.VMEM((width, hidden), BF),
            pltpu.VMEM((1, hidden), F32),
            pltpu.VMEM((steps, block, received_rows), BF),
            pltpu.VMEM((steps, block, hubs), BF),
            pltpu.VMEM((steps, block, width), BF),
            pltpu.VMEM((steps, block, hidden), BF),
            pltpu.VMEM((steps, block, 2 * width), F32),
            pltpu.VMEM((received_rows, width), BF),
            pltpu.VMEM((width, nodes), BF),
            pltpu.VMEM((steps, block, hidden), BF),
            pltpu.VMEM((rows, depth, width), BF),
            pltpu.VMEM((1, hidden), F32),
            pltpu.VMEM((width, hubs), F32),
            pltpu.VMEM((2 * width, hidden), F32),
            sems(4 + 5 * steps),
            sems(2 * steps + 2),
        ],
    )(
        w_self,
        w_neigh,
        bias.reshape(1, hidden),
        boundary_adj,
        hub_adj,
        features,
        cotangent,
        ext,
        received,
    )
    first = swap(first, "row")

    back = call(
        boundary_back_kernel,
        "boundary_back",
        struct((peers, slots, width), BF),
        2 * nodes * received_rows * width,
        nodes * received_rows * 2,
        in_specs=[HBM, VMEM],
        scratch_shapes=[
            pltpu.VMEM((steps, block, received_rows), BF),
            pltpu.VMEM((width, received_rows), F32),
            sems(steps),
        ],
    )(boundary_adj, grad_t)

    base = call(
        local_back_kernel,
        "local_back",
        struct((nodes, width), F32),
        2 * tiles * side * side * width + 2 * nodes * width * hidden,
        tiles * side * side * 2 + nodes * width * 10,
        in_specs=[HBM, HBM, HBM, VMEM, VMEM],
        scratch_shapes=[
            pltpu.SMEM((2, tiles), int32),
            pltpu.VMEM((width, hidden), BF),
            pltpu.VMEM((tile_steps, tile_block, side, side), BF),
            pltpu.VMEM((nodes // side, width, side), F32),
            sems(2 + tile_steps),
        ],
    )(tile_index, w_self, local_tiles, grad_t, pg)

    hub_mine, second = call(
        row_sum_kernel,
        "row_sum",
        (struct((4 * hub_own, width), BF), struct((peers, slots + 48, width), BF)),
        rows * depth * width,
        rows * depth * width * 2 + peers * slots * width * 4,
    )(first, back, bias_sum)
    second = swap(second, "col")

    third = call(
        col_sum_kernel,
        "col_sum",
        struct((rows, 24, width), F32),
        peers * 48 * width,
        peers * slots * width * 4,
    )(second)
    third = swap(third, "row")

    slot = jnp.arange(slots, dtype=jnp.int32)[None, :]
    listed = jnp.where(slot < send_counts[:, None], send_rows, -1)
    unused = jnp.full((1, slots - 3 * hub_own), -1, jnp.int32)
    hub_slots = jnp.concatenate([hub_rows, hub_rows, hub_rows, unused], axis=1)
    index = jnp.concatenate([listed, hub_slots], axis=0)
    index = jnp.pad(index, ((0, 16 - index.shape[0]), (0, 0)), constant_values=-1)
    grad_features = call(
        scatter_kernel,
        "scatter",
        struct((nodes, width), BF),
        2 * nodes * received_rows * width,
        nodes * width * 6 + received_rows * width * 2,
        grid=(steps,),
        in_specs=[
            whole((16, slots)),
            whole((peers, slots + 48, width)),
            whole((4 * hub_own, width)),
            pl.BlockSpec((block, width), lambda i: (i, 0)),
        ],
        out_specs=pl.BlockSpec((block, width), lambda i: (i, 0)),
    )(index, second, hub_mine, base)

    factor = 1.0 / math.sqrt(nodes * rows * cols)

    def finish(*refs):
        finish_kernel(*refs, factor=factor)

    grad_self, grad_neigh, grad_bias = call(
        finish,
        "finish",
        (struct((width, hidden), F32), struct((width, hidden), F32), struct((1, hidden), F32)),
        rows * 24 * width,
        rows * 24 * width * 4,
    )(third)
    return grad_features, grad_self, grad_neigh, grad_bias.reshape(hidden)


def solution(mesh):
    placed = (
        P(("row", "col"), None),
        P(),
        P(),
        P(),
        P(("row", "col"), None),
        P(("row", "col"), None, None),
        P(("row", "col"), None),
        P(("row", "col"), None),
        P(("row", "col"), None),
        P(("row", "col")),
        P(("row", "col"), None),
        P(("row", "col"), None),
    )
    return jax.shard_map(
        body,
        mesh=mesh,
        in_specs=placed,
        out_specs=(P(("row", "col"), None), P(), P(), P()),
        check_vma=False,
    )
```

```python
import math

import jax
import jax.numpy as jnp
from jax import lax
from jax.experimental import pallas as pl
from jax.experimental.pallas import tpu as pltpu
from jax.sharding import PartitionSpec as P

BF = jnp.bfloat16
F32 = jnp.float32
LANES = 128
MIB = 1 << 20


def mm(left, right):
    return jnp.dot(left, right, preferred_element_type=F32)


def with_ones(rows):
    return jnp.concatenate([rows, jnp.ones((rows.shape[0], LANES), BF)], axis=1)


def column(row):
    n = row.shape[1]
    down = lax.broadcasted_iota(jnp.int32, (n, n), 0)
    across = lax.broadcasted_iota(jnp.int32, (n, n), 1)
    picked = jnp.where(down == across, row.astype(F32), 0.0)
    return jnp.sum(picked, axis=1, keepdims=True).astype(jnp.int32)


def onehot(match):
    return jnp.where(match, 1.0, 0.0).astype(BF)


def call(kernel, name, out, flops, nbytes, vmem=24, **rest):
    return pl.pallas_call(
        kernel,
        out_shape=out,
        name=name,
        cost_estimate=pl.CostEstimate(flops=flops, bytes_accessed=nbytes, transcendentals=0),
        compiler_params=pltpu.CompilerParams(vmem_limit_bytes=vmem * MIB),
        **rest,
    )


def whole(shape):
    return pl.BlockSpec(shape, lambda *_: (0,) * len(shape))


HBM = pl.BlockSpec(memory_space=pltpu.HBM)
VMEM = pl.BlockSpec(memory_space=pltpu.VMEM)


def fetch(source, target, sem):
    copy = pltpu.make_async_copy(source, target, sem)
    copy.start()
    return copy


def chunks(ref, buf, sems, first):
    size = buf.shape[1]
    return [
        fetch(ref.at[pl.ds(i * size, size)], buf.at[i], sems.at[first + i])
        for i in range(buf.shape[0])
    ]


def hub_rows_kernel(rows_hbm, feat_hbm, out_ref, rows_ref, feat_ref, sems):
    listed = fetch(rows_hbm, rows_ref, sems.at[0])
    feat = fetch(feat_hbm, feat_ref, sems.at[1])
    listed.wait()
    nodes = feat_ref.shape[0]
    lanes = lax.broadcasted_iota(jnp.int32, (rows_ref.shape[1], nodes), 1)
    pick = onehot(lanes == column(rows_ref[...]))
    feat.wait()
    own = mm(pick, feat_ref[...]).astype(BF)
    out_ref[...] = jnp.broadcast_to(own[None], out_ref.shape)


def send_kernel(counts_hbm, rows_hbm, feat_hbm, out_ref, counts_ref, rows_ref, feat_ref, sems):
    counts = fetch(counts_hbm, counts_ref, sems.at[0])
    listed_rows = fetch(rows_hbm, rows_ref, sems.at[1])
    feat = fetch(feat_hbm, feat_ref, sems.at[2])
    counts.wait()
    listed_rows.wait()
    feat.wait()
    nodes = feat_ref.shape[0]
    peers, slots = rows_ref.shape
    lanes = lax.broadcasted_iota(jnp.int32, (slots, nodes), 1)
    slot = lax.broadcasted_iota(jnp.int32, (1, slots), 1)
    for peer in range(peers):
        listed = jnp.where(slot < counts_ref[peer], rows_ref[peer : peer + 1, :], -1)
        out_ref[peer] = mm(onehot(lanes == column(listed)), feat_ref[...]).astype(BF)


def local_kernel(
    idx_hbm, feat_hbm, tiles_hbm, ext_hbm, idx_ref, feat_ref, tiles_ref, acc, sems, out_sem
):
    index = fetch(idx_hbm, idx_ref, sems.at[0])
    feat = fetch(feat_hbm, feat_ref, sems.at[1])
    parts = chunks(tiles_hbm, tiles_ref, sems, 2)
    steps, count, side, _ = tiles_ref.shape
    acc[...] = jnp.zeros_like(acc)
    index.wait()
    feat.wait()
    for step in range(steps):
        parts[step].wait()
        for t in range(count):
            k = step * count + t
            to = pl.multiple_of(idx_ref[0, k] * side, side)
            at = pl.multiple_of(idx_ref[1, k] * side, side)
            rows = with_ones(feat_ref[pl.ds(at, side), :])
            acc[pl.ds(to, side), :] += mm(tiles_ref[step, t], rows)
    fetch(acc, ext_hbm, out_sem.at[0]).wait()


def boundary_kernel(
    received_hbm, adj_hbm, local_hbm, ext_hbm, received_ref, adj_ref, acc, sems, out_sems
):
    received_copy = fetch(received_hbm, received_ref, sems.at[0])
    steps, block, _ = adj_ref.shape
    parts = [
        (
            fetch(adj_hbm.at[pl.ds(i * block, block)], adj_ref.at[i], sems.at[1 + 2 * i]),
            fetch(local_hbm.at[pl.ds(i * block, block)], acc.at[i], sems.at[2 + 2 * i]),
        )
        for i in range(steps)
    ]
    received_copy.wait()
    received = with_ones(received_ref[...])
    stores = []
    for i in range(steps):
        for copy in parts[i]:
            copy.wait()
        acc[i] += mm(adj_ref[i], received)
        stores.append(fetch(acc.at[i], ext_hbm.at[pl.ds(i * block, block)], out_sems.at[i]))
    for store in stores:
        store.wait()


def middle_kernel(
    w_self_hbm,
    w_neigh_hbm,
    bias_hbm,
    hub_hbm,
    feat_hbm,
    cot_hbm,
    ext_hbm,
    table_hbm,
    grad_t_hbm,
    pg_hbm,
    first_hbm,
    bias_sum_hbm,
    w_self_ref,
    w_neigh_ref,
    bias_ref,
    hub_ref,
    feat_ref,
    cot_ref,
    ext_ref,
    table_ref,
    grad_t_ref,
    pg_ref,
    first_ref,
    bias_sum,
    hub_acc,
    w_acc,
    sems,
    out_sems,
):
    steps, block, width = feat_ref.shape
    small = [
        fetch(table_hbm, table_ref, sems.at[3]),
        fetch(w_self_hbm, w_self_ref, sems.at[0]),
        fetch(w_neigh_hbm, w_neigh_ref, sems.at[1]),
        fetch(bias_hbm, bias_ref, sems.at[2]),
    ]
    pairs = (
        (hub_hbm, hub_ref),
        (ext_hbm, ext_ref),
        (feat_hbm, feat_ref),
        (cot_hbm, cot_ref),
    )
    large = []
    for i in range(steps):
        rows = pl.ds(i * block, block)
        large.append(
            [
                fetch(source.at[rows], target.at[i], sems.at[4 + 4 * i + j])
                for j, (source, target) in enumerate(pairs)
            ]
        )
    for copy in small:
        copy.wait()
    table = with_ones(table_ref[...])
    w_both = jnp.concatenate([w_self_ref[...], w_neigh_ref[...]], axis=0)
    stores = []
    done = None
    for i in range(steps + 1):
        if i < steps:
            for copy in large[i]:
                copy.wait()
            rows = pl.ds(i * block, block)
            ext = ext_ref[i] + mm(hub_ref[i], table)
            inverse = 1.0 / (1.0 + ext[:, width:])
            mean = (ext[:, :width] * inverse).astype(BF)
            both = jnp.concatenate([feat_ref[i], mean], axis=1)
            preact = mm(both, w_both) + bias_ref[...]
            slope = jnp.where(preact > 0, 1.0, jnp.exp(jnp.minimum(preact, 0.0)))
            pg = (cot_ref[i].astype(F32) * slope).astype(BF)
            pg_ref[i] = pg
            grad = lax.dot_general(
                pg, w_neigh_ref[...], (((1,), (1,)), ((), ())), preferred_element_type=F32
            )
            grad_t = jnp.transpose(grad * inverse).astype(BF)
            grad_t_ref[:, rows] = grad_t
        if i > 0:
            last_both, last_pg, last_grad_t = done
            hub_part = mm(last_grad_t, hub_ref[i - 1])
            w_part = mm(jnp.transpose(last_both), last_pg)
            bias_part = jnp.sum(last_pg.astype(F32), axis=0, keepdims=True)
            if i == 1:
                hub_acc[...] = hub_part
                w_acc[...] = w_part
                bias_sum[...] = bias_part
            else:
                hub_acc[...] += hub_part
                w_acc[...] += w_part
                bias_sum[...] += bias_part
        if i < steps:
            done = (both, pg, grad_t)
            stores.append(fetch(pg_ref.at[i], pg_hbm.at[rows], out_sems.at[2 * i]))
            stores.append(
                fetch(grad_t_ref.at[:, rows], grad_t_hbm.at[:, rows], out_sems.at[2 * i + 1])
            )
    rows, depth, _ = first_ref.shape
    hubs = hub_acc.shape[1] // rows
    share = w_acc.shape[0] // rows
    hub_back = jnp.transpose(hub_acc[...]).astype(BF)
    first_ref[:, :hubs, :] = hub_back.reshape(rows, hubs, width)
    left = w_acc[:, :LANES].reshape(rows, share, LANES)
    right = w_acc[:, LANES:].reshape(rows, share, LANES)
    first_ref[:, hubs:, :] = jnp.concatenate([left, right], axis=1).astype(BF)
    stores.append(fetch(first_ref, first_hbm, out_sems.at[2 * steps]))
    stores.append(fetch(bias_sum, bias_sum_hbm, out_sems.at[2 * steps + 1]))
    for store in stores:
        store.wait()


def boundary_back_kernel(bound_hbm, grad_t_ref, out_ref, bound_ref, acc, sems):
    parts = chunks(bound_hbm, bound_ref, sems, 0)
    steps, block, _ = bound_ref.shape
    for i in range(steps):
        parts[i].wait()
        part = mm(grad_t_ref[:, pl.ds(i * block, block)], bound_ref[i])
        if i == 0:
            acc[...] = part
        else:
            acc[...] += part
    out_ref[...] = jnp.transpose(acc[...]).astype(BF).reshape(out_ref.shape)


def local_back_kernel(
    idx_hbm,
    w_self_hbm,
    tiles_hbm,
    grad_t_ref,
    pg_ref,
    out_ref,
    idx_ref,
    w_self_ref,
    tiles_ref,
    acc,
    sems,
):
    index = fetch(idx_hbm, idx_ref, sems.at[0])
    weights = fetch(w_self_hbm, w_self_ref, sems.at[1])
    parts = chunks(tiles_hbm, tiles_ref, sems, 2)
    acc[...] = jnp.zeros_like(acc)
    steps, count, side, _ = tiles_ref.shape
    index.wait()
    weights.wait()
    for step in range(steps):
        parts[step].wait()
        for t in range(count):
            k = step * count + t
            at = pl.multiple_of(idx_ref[0, k] * side, side)
            acc[idx_ref[1, k]] += mm(grad_t_ref[:, pl.ds(at, side)], tiles_ref[step, t])
    for b in range(acc.shape[0]):
        rows = pl.ds(b * side, side)
        own = lax.dot_general(
            pg_ref[rows, :],
            w_self_ref[...],
            (((1,), (1,)), ((), ())),
            preferred_element_type=F32,
        )
        out_ref[rows, :] = own + jnp.transpose(acc[b])


def split(value):
    high = value.astype(BF)
    return high, (value - high.astype(F32)).astype(BF)


def row_sum_kernel(first_ref, back_ref, bias_ref, hub_ref, second_ref):
    rows, depth, width = first_ref.shape
    total = first_ref[0].astype(F32)
    for r in range(1, rows):
        total += first_ref[r].astype(F32)
    hubs = depth - 16
    hub = total[:hubs]
    high, rest = split(hub)
    middle, low = split(hub - high.astype(F32))
    hub_ref[...] = jnp.concatenate([high, middle, low, jnp.zeros((hubs, width), BF)], axis=0)
    peers, _, _ = second_ref.shape
    slots = back_ref.shape[1]
    w_high, w_low = split(total[hubs:])
    bias = jnp.concatenate([bias_ref[:, :width], bias_ref[:, width:]], axis=0)
    b_rest = bias - bias.astype(BF).astype(F32)
    b_rows = jnp.concatenate([bias, b_rest, jnp.zeros((12, width), F32)], axis=0).astype(BF)
    for p in range(peers):
        second_ref[p, :slots] = back_ref[p]
        second_ref[p, slots : slots + 16] = w_high
        second_ref[p, slots + 16 : slots + 32] = w_low
        second_ref[p, slots + 32 : slots + 48] = b_rows


def col_sum_kernel(second_ref, third_ref):
    peers, depth, width = second_ref.shape
    start = depth - 48
    total = second_ref[0, start:].astype(F32)
    for p in range(1, peers):
        total += second_ref[p, start:].astype(F32)
    weights = total[:16] + total[16:32]
    bias = total[32:34] + total[34:36]
    rest = bias - bias.astype(BF).astype(F32)
    done = jnp.concatenate([weights, bias, rest, jnp.zeros((4, width), F32)], axis=0).astype(BF)
    third_ref[...] = jnp.broadcast_to(done[None], third_ref.shape)


def scatter_kernel(idx_ref, second_ref, hub_ref, base_ref, out_ref):
    block = out_ref.shape[0]
    peers = second_ref.shape[0]
    slots = idx_ref.shape[1]
    node = lax.broadcasted_iota(jnp.int32, (block, slots), 0) + pl.program_id(0) * block
    match = [onehot(node == idx_ref[p : p + 1, :]) for p in range(peers + 1)]
    values = [second_ref[p, :slots, :] for p in range(peers)] + [hub_ref[...]]
    added = mm(jnp.concatenate(match, axis=1), jnp.concatenate(values, axis=0))
    out_ref[...] = (base_ref[...] + added).astype(BF)


def finish_kernel(third_ref, self_ref, neigh_ref, bias_ref, *, factor):
    rows = third_ref.shape[0]
    share = 8
    third = third_ref[...].astype(F32)
    left = third[:, :share, :].reshape(rows * share, LANES)
    right = third[:, share : 2 * share, :].reshape(rows * share, LANES)
    grads = jnp.concatenate([left, right], axis=1) * factor
    half = grads.shape[0] // 2
    self_ref[...] = grads[:half]
    neigh_ref[...] = grads[half:]
    bias = third[0, 16:24, :]
    for r in range(1, rows):
        bias += third[r, 16:24, :]
    bias = bias[0:2] + bias[2:4]
    bias_ref[...] = jnp.concatenate([bias[0:1], bias[1:2]], axis=1) * factor


def swap(parts, axis):
    return lax.all_to_all(parts, axis, split_axis=0, concat_axis=0, tiled=True)


def body(
    features,
    w_self,
    w_neigh,
    bias,
    cotangent,
    local_tiles,
    local_tile_idx,
    boundary_adj,
    send_rows,
    send_counts,
    hub_adj,
    hub_rows,
):
    nodes, width = features.shape
    hidden = w_self.shape[1]
    tiles, side, _ = local_tiles.shape
    peers, slots = send_rows.shape
    hub_own = hub_rows.shape[1]
    rows = lax.axis_size("row")
    cols = lax.axis_size("col")
    hubs = rows * hub_own
    received_rows = peers * slots
    struct = jax.ShapeDtypeStruct
    block = 512
    steps = nodes // block
    tile_steps = 4
    tile_block = tiles // tile_steps

    tile_index = local_tile_idx.T
    sems = lambda count: pltpu.SemaphoreType.DMA((count,))
    int32 = jnp.int32

    outgoing = call(
        send_kernel,
        "send_rows",
        struct((peers, slots, width), BF),
        2 * peers * slots * nodes * width,
        nodes * width * 2,
        vmem=60,
        in_specs=[HBM, HBM, HBM],
        scratch_shapes=[
            pltpu.SMEM((peers,), int32),
            pltpu.VMEM((peers, slots), int32),
            pltpu.VMEM((nodes, width), BF),
            sems(3),
        ],
    )(send_counts, send_rows, features)
    received = swap(outgoing, "col").reshape(received_rows, width)

    hub_send = call(
        hub_rows_kernel,
        "hub_rows",
        struct((rows, hub_own, width), BF),
        2 * hub_own * nodes * width,
        nodes * width * 2,
        vmem=60,
        in_specs=[HBM, HBM],
        scratch_shapes=[
            pltpu.VMEM((1, hub_own), int32),
            pltpu.VMEM((nodes, width), BF),
            sems(2),
        ],
    )(hub_rows, features)
    local = call(
        local_kernel,
        "local_forward",
        struct((nodes, 2 * width), F32),
        4 * tiles * side * side * width,
        tiles * side * side * 2 + nodes * width * 10,
        vmem=60,
        in_specs=[HBM] * 3,
        out_specs=HBM,
        scratch_shapes=[
            pltpu.SMEM((2, tiles), int32),
            pltpu.VMEM((nodes, width), BF),
            pltpu.VMEM((tile_steps, tile_block, side, side), BF),
            pltpu.VMEM((nodes, 2 * width), F32),
            sems(2 + tile_steps),
            sems(1),
        ],
    )(tile_index, features, local_tiles)

    hub_send, received, local = lax.optimization_barrier((hub_send, received, local))
    table = swap(hub_send, "row").reshape(hubs, width)

    ext = call(
        boundary_kernel,
        "boundary_forward",
        struct((nodes, 2 * width), F32),
        4 * nodes * received_rows * width,
        nodes * width * 16 + nodes * received_rows * 2,
        vmem=60,
        in_specs=[HBM] * 3,
        out_specs=HBM,
        scratch_shapes=[
            pltpu.VMEM((received_rows, width), BF),
            pltpu.VMEM((steps, block, received_rows), BF),
            pltpu.VMEM((steps, block, 2 * width), F32),
            sems(1 + 2 * steps),
            sems(steps),
        ],
    )(received, boundary_adj, local)

    share = 2 * width // rows
    depth = hub_own + 2 * share
    grad_t, pg, first, bias_sum = call(
        middle_kernel,
        "middle",
        (
            struct((width, nodes), BF),
            struct((nodes, hidden), BF),
            struct((rows, depth, width), BF),
            struct((1, hidden), F32),
        ),
        8 * nodes * hubs * width,
        nodes * (hubs * 4 + width * 16),
        vmem=60,
        in_specs=[HBM] * 8,
        out_specs=(HBM,) * 4,
        scratch_shapes=[
            pltpu.VMEM((width, hidden), BF),
            pltpu.VMEM((width, hidden), BF),
            pltpu.VMEM((1, hidden), F32),
            pltpu.VMEM((steps, block, hubs), BF),
            pltpu.VMEM((steps, block, width), BF),
            pltpu.VMEM((steps, block, hidden), BF),
            pltpu.VMEM((steps, block, 2 * width), F32),
            pltpu.VMEM((hubs, width), BF),
            pltpu.VMEM((width, nodes), BF),
            pltpu.VMEM((steps, block, hidden), BF),
            pltpu.VMEM((rows, depth, width), BF),
            pltpu.VMEM((1, hidden), F32),
            pltpu.VMEM((width, hubs), F32),
            pltpu.VMEM((2 * width, hidden), F32),
            sems(4 + 4 * steps),
            sems(2 * steps + 2),
        ],
    )(
        w_self,
        w_neigh,
        bias.reshape(1, hidden),
        hub_adj,
        features,
        cotangent,
        ext,
        table,
    )
    first = swap(first, "row")

    back = call(
        boundary_back_kernel,
        "boundary_back",
        struct((peers, slots, width), BF),
        2 * nodes * received_rows * width,
        nodes * received_rows * 2,
        in_specs=[HBM, VMEM],
        scratch_shapes=[
            pltpu.VMEM((steps, block, received_rows), BF),
            pltpu.VMEM((width, received_rows), F32),
            sems(steps),
        ],
    )(boundary_adj, grad_t)

    base = call(
        local_back_kernel,
        "local_back",
        struct((nodes, width), F32),
        2 * tiles * side * side * width + 2 * nodes * width * hidden,
        tiles * side * side * 2 + nodes * width * 10,
        in_specs=[HBM, HBM, HBM, VMEM, VMEM],
        scratch_shapes=[
            pltpu.SMEM((2, tiles), int32),
            pltpu.VMEM((width, hidden), BF),
            pltpu.VMEM((tile_steps, tile_block, side, side), BF),
            pltpu.VMEM((nodes // side, width, side), F32),
            sems(2 + tile_steps),
        ],
    )(tile_index, w_self, local_tiles, grad_t, pg)

    first, back, base = lax.optimization_barrier((first, back, base))
    hub_mine, second = call(
        row_sum_kernel,
        "row_sum",
        (struct((4 * hub_own, width), BF), struct((peers, slots + 48, width), BF)),
        rows * depth * width,
        rows * depth * width * 2 + peers * slots * width * 4,
    )(first, back, bias_sum)
    second = swap(second, "col")

    third = call(
        col_sum_kernel,
        "col_sum",
        struct((rows, 24, width), BF),
        cols * 24 * width,
        cols * 24 * width * 4,
    )(second)
    third = swap(third, "row")

    slot = jnp.arange(slots, dtype=jnp.int32)[None, :]
    listed = jnp.where(slot < send_counts[:, None], send_rows, -1)
    unused = jnp.full((1, slots - 3 * hub_own), -1, jnp.int32)
    hub_slots = jnp.concatenate([hub_rows, hub_rows, hub_rows, unused], axis=1)
    index = jnp.concatenate([listed, hub_slots], axis=0)
    index = jnp.pad(index, ((0, 16 - index.shape[0]), (0, 0)), constant_values=-1)
    grad_features = call(
        scatter_kernel,
        "scatter",
        struct((nodes, width), BF),
        2 * nodes * received_rows * width,
        nodes * width * 6 + received_rows * width * 2,
        grid=(steps,),
        in_specs=[
            whole((16, slots)),
            whole((peers, slots + 48, width)),
            whole((4 * hub_own, width)),
            pl.BlockSpec((block, width), lambda i: (i, 0)),
        ],
        out_specs=pl.BlockSpec((block, width), lambda i: (i, 0)),
    )(index, second, hub_mine, base)

    factor = 1.0 / math.sqrt(nodes * rows * cols)

    def finish(*refs):
        finish_kernel(*refs, factor=factor)

    grad_self, grad_neigh, grad_bias = call(
        finish,
        "finish",
        (struct((width, hidden), F32), struct((width, hidden), F32), struct((1, hidden), F32)),
        rows * 24 * width,
        rows * 24 * width * 4,
    )(third)
    return grad_features, grad_self, grad_neigh, grad_bias.reshape(hidden)


def solution(mesh):
    placed = (
        P(("row", "col"), None),
        P(),
        P(),
        P(),
        P(("row", "col"), None),
        P(("row", "col"), None, None),
        P(("row", "col"), None),
        P(("row", "col"), None),
        P(("row", "col"), None),
        P(("row", "col")),
        P(("row", "col"), None),
        P(("row", "col"), None),
    )
    return jax.shard_map(
        body,
        mesh=mesh,
        in_specs=placed,
        out_specs=(P(("row", "col"), None), P(), P(), P()),
        check_vma=False,
    )
```

```python
import math

import jax
import jax.numpy as jnp
from jax import lax
from jax.experimental import pallas as pl
from jax.experimental.pallas import tpu as pltpu
from jax.sharding import PartitionSpec as P

BF = jnp.bfloat16
F32 = jnp.float32
LANES = 128
MIB = 1 << 20


def mm(left, right):
    return jnp.dot(left, right, preferred_element_type=F32)


def with_ones(rows):
    return jnp.concatenate([rows, jnp.ones((rows.shape[0], LANES), BF)], axis=1)


def column(row):
    n = row.shape[1]
    down = lax.broadcasted_iota(jnp.int32, (n, n), 0)
    across = lax.broadcasted_iota(jnp.int32, (n, n), 1)
    picked = jnp.where(down == across, row.astype(F32), 0.0)
    return jnp.sum(picked, axis=1, keepdims=True).astype(jnp.int32)


def onehot(match):
    return jnp.where(match, 1.0, 0.0).astype(BF)


def call(kernel, name, out, flops, nbytes, vmem=24, **rest):
    return pl.pallas_call(
        kernel,
        out_shape=out,
        name=name,
        cost_estimate=pl.CostEstimate(flops=flops, bytes_accessed=nbytes, transcendentals=0),
        compiler_params=pltpu.CompilerParams(vmem_limit_bytes=vmem * MIB),
        **rest,
    )


def whole(shape):
    return pl.BlockSpec(shape, lambda *_: (0,) * len(shape))


HBM = pl.BlockSpec(memory_space=pltpu.HBM)
VMEM = pl.BlockSpec(memory_space=pltpu.VMEM)


def fetch(source, target, sem):
    copy = pltpu.make_async_copy(source, target, sem)
    copy.start()
    return copy


def chunks(ref, buf, sems, first):
    size = buf.shape[1]
    return [
        fetch(ref.at[pl.ds(i * size, size)], buf.at[i], sems.at[first + i])
        for i in range(buf.shape[0])
    ]


def gather_kernel(
    counts_hbm, rows_hbm, hubs_hbm, feat_hbm, hub_ref, *rest
):
    *send_refs, counts_ref, rows_ref, hubs_ref, feat_ref, sems = rest
    copies = [
        fetch(source, target, sems.at[i])
        for i, (source, target) in enumerate(
            (
                (hubs_hbm, hubs_ref),
                (feat_hbm, feat_ref),
                (counts_hbm, counts_ref),
                (rows_hbm, rows_ref),
            )
        )
    ]
    for copy in copies:
        copy.wait()
    nodes = feat_ref.shape[0]
    slots = rows_ref.shape[1]
    lanes = lax.broadcasted_iota(jnp.int32, (slots, nodes), 1)
    slot = lax.broadcasted_iota(jnp.int32, (1, slots), 1)
    pick = onehot(lanes[: hubs_ref.shape[1]] == column(hubs_ref[...]))
    own = mm(pick, feat_ref[...]).astype(BF)
    hub_ref[...] = jnp.broadcast_to(own[None], hub_ref.shape)
    for ref, e, k in departures(*send_refs):
        peer = peer_of(e, k)
        listed = jnp.where(slot < counts_ref[peer], rows_ref[pl.ds(peer, 1), :], -1)
        ref[...] = mm(onehot(lanes == column(listed)), feat_ref[...]).astype(BF)


def middle_kernel(
    w_self_hbm,
    w_neigh_hbm,
    bias_hbm,
    bound_hbm,
    hub_hbm,
    feat_hbm,
    cot_hbm,
    idx_hbm,
    tiles_hbm,
    table_hbm,
    parts_hbm,
    grad_t_hbm,
    pg_hbm,
    first_hbm,
    bias_sum_hbm,
    back_hbm,
    w_self_ref,
    w_neigh_ref,
    bias_ref,
    bound_ref,
    hub_ref,
    feat_ref,
    cot_ref,
    idx_ref,
    tiles_ref,
    ext_ref,
    received_ref,
    table_ref,
    grad_t_ref,
    pg_ref,
    first_ref,
    bias_sum,
    back_refs,
    back_acc,
    hub_acc,
    w_acc,
    sems,
    out_sems,
):
    nodes, width = feat_ref.shape
    steps, block, _ = cot_ref.shape
    tile_steps, count, side, _ = tiles_ref.shape
    index = fetch(idx_hbm, idx_ref, sems.at[4])
    feat = fetch(feat_hbm, feat_ref, sems.at[5])
    tile_parts = chunks(tiles_hbm, tiles_ref, sems, 6)
    at_large = 6 + tile_steps
    small = [
        fetch(table_hbm, table_ref, sems.at[3]),
        fetch(w_self_hbm, w_self_ref, sems.at[0]),
        fetch(w_neigh_hbm, w_neigh_ref, sems.at[1]),
        fetch(bias_hbm, bias_ref, sems.at[2]),
    ]
    slots = parts_hbm[0].shape[0]
    for n, (source, e, k) in enumerate(arrivals(*parts_hbm)):
        to = received_ref.at[pl.ds(pl.multiple_of(peer_of(e, k) * slots, slots), slots)]
        small.append(fetch(source, to, sems.at[at_large + 3 * steps + n]))
    pairs = (
        (bound_hbm, bound_ref),
        (cot_hbm, cot_ref),
        (hub_hbm, hub_ref),
    )
    large = []
    for i in range(steps):
        rows = pl.ds(i * block, block)
        large.append(
            [
                fetch(source.at[rows], target.at[i], sems.at[at_large + 3 * i + j])
                for j, (source, target) in enumerate(pairs)
            ]
        )
    ext_ref[...] = jnp.zeros_like(ext_ref)
    index.wait()
    feat.wait()
    for step in range(tile_steps):
        tile_parts[step].wait()
        for t in range(count):
            k = step * count + t
            to = pl.multiple_of(idx_ref[0, k] * side, side)
            at = pl.multiple_of(idx_ref[1, k] * side, side)
            rows = with_ones(feat_ref[pl.ds(at, side), :])
            ext_ref[pl.ds(to, side), :] += mm(tiles_ref[step, t], rows)
    for copy in small:
        copy.wait()
    received = with_ones(received_ref[...])
    table = with_ones(table_ref[...])
    w_both = jnp.concatenate([w_self_ref[...], w_neigh_ref[...]], axis=0)
    stores = []
    done = None
    for i in range(steps + 1):
        if i < steps:
            for copy in large[i]:
                copy.wait()
            rows = pl.ds(i * block, block)
            ext = ext_ref[rows, :] + mm(bound_ref[i], received) + mm(hub_ref[i], table)
            inverse = 1.0 / (1.0 + ext[:, width:])
            mean = (ext[:, :width] * inverse).astype(BF)
            both = jnp.concatenate([feat_ref[rows, :], mean], axis=1)
            preact = mm(both, w_both) + bias_ref[...]
            slope = jnp.where(preact > 0, 1.0, jnp.exp(jnp.minimum(preact, 0.0)))
            pg = (cot_ref[i].astype(F32) * slope).astype(BF)
            pg_ref[i] = pg
            grad = lax.dot_general(
                pg, w_neigh_ref[...], (((1,), (1,)), ((), ())), preferred_element_type=F32
            )
            grad_t = jnp.transpose(grad * inverse).astype(BF)
            grad_t_ref[:, rows] = grad_t
        if i > 0:
            last_both, last_pg, last_grad_t = done
            back_part = mm(last_grad_t, bound_ref[i - 1])
            hub_part = mm(last_grad_t, hub_ref[i - 1])
            w_part = mm(jnp.transpose(last_both), last_pg)
            bias_part = jnp.sum(last_pg.astype(F32), axis=0, keepdims=True)
            if i == 1:
                back_acc[...] = back_part
                hub_acc[...] = hub_part
                w_acc[...] = w_part
                bias_sum[...] = bias_part
            else:
                back_acc[...] += back_part
                hub_acc[...] += hub_part
                w_acc[...] += w_part
                bias_sum[...] += bias_part
        if i < steps:
            done = (both, pg, grad_t)
            stores.append(fetch(pg_ref.at[i], pg_hbm.at[rows], out_sems.at[2 * i]))
            stores.append(
                fetch(grad_t_ref.at[:, rows], grad_t_hbm.at[:, rows], out_sems.at[2 * i + 1])
            )
    rows, depth, _ = first_ref.shape
    hubs = hub_acc.shape[1] // rows
    share = w_acc.shape[0] // rows
    hub_back = jnp.transpose(hub_acc[...]).astype(BF)
    first_ref[:, :hubs, :] = hub_back.reshape(rows, hubs, width)
    left = w_acc[:, :LANES].reshape(rows, share, LANES)
    right = w_acc[:, LANES:].reshape(rows, share, LANES)
    first_ref[:, hubs:, :] = jnp.concatenate([left, right], axis=1).astype(BF)
    stores.append(fetch(first_ref, first_hbm, out_sems.at[2 * steps]))
    stores.append(fetch(bias_sum, bias_sum_hbm, out_sems.at[2 * steps + 1]))
    for ref, e, k in departures(*back_refs):
        at = pl.multiple_of(peer_of(e, k) * LANES, LANES)
        ref[...] = jnp.transpose(back_acc[:, pl.ds(at, LANES)]).astype(BF)
    for n, (source, target) in enumerate(zip(back_refs, back_hbm)):
        stores.append(fetch(source, target, out_sems.at[2 * steps + 2 + n]))
    for store in stores:
        store.wait()


def local_back_kernel(
    idx_hbm,
    w_self_hbm,
    tiles_hbm,
    grad_t_ref,
    pg_ref,
    out_ref,
    idx_ref,
    w_self_ref,
    tiles_ref,
    acc,
    sems,
):
    index = fetch(idx_hbm, idx_ref, sems.at[0])
    weights = fetch(w_self_hbm, w_self_ref, sems.at[1])
    parts = chunks(tiles_hbm, tiles_ref, sems, 2)
    acc[...] = jnp.zeros_like(acc)
    steps, count, side, _ = tiles_ref.shape
    index.wait()
    weights.wait()
    for step in range(steps):
        parts[step].wait()
        for t in range(count):
            k = step * count + t
            at = pl.multiple_of(idx_ref[0, k] * side, side)
            acc[idx_ref[1, k]] += mm(grad_t_ref[:, pl.ds(at, side)], tiles_ref[step, t])
    for b in range(acc.shape[0]):
        rows = pl.ds(b * side, side)
        own = lax.dot_general(
            pg_ref[rows, :],
            w_self_ref[...],
            (((1,), (1,)), ((), ())),
            preferred_element_type=F32,
        )
        out_ref[rows, :] = own + jnp.transpose(acc[b])


def row_sum_kernel(first_ref, bias_ref, hub_ref, second_ref):
    rows, depth, width = first_ref.shape
    total = first_ref[0].astype(F32)
    for r in range(1, rows):
        total += first_ref[r].astype(F32)
    hubs = depth - 16
    hub = total[:hubs]
    high = hub.astype(BF)
    rest = hub - high.astype(F32)
    middle = rest.astype(BF)
    low = (rest - middle.astype(F32)).astype(BF)
    hub_ref[...] = jnp.concatenate([high, middle, low, jnp.zeros((hubs, width), BF)], axis=0)
    bias = jnp.concatenate([bias_ref[:, :width], bias_ref[:, width:]], axis=0)
    mine = jnp.concatenate([total[hubs:], bias, jnp.zeros((6, width), F32)], axis=0)
    second_ref[...] = jnp.broadcast_to(mine[None], second_ref.shape)


def col_sum_kernel(second_ref, third_ref):
    total = second_ref[0]
    for p in range(1, second_ref.shape[0]):
        total += second_ref[p]
    bias = total[16:18]
    rest = bias - bias.astype(BF).astype(F32)
    done = jnp.concatenate([total[:18], rest, total[20:]], axis=0).astype(BF)
    third_ref[...] = jnp.broadcast_to(done[None], third_ref.shape)


def scatter_kernel(idx_ref, hub_ref, base_ref, *refs):
    *parts, out_ref = refs
    block = out_ref.shape[0]
    slots = idx_ref.shape[1]
    blocks = arrivals(*parts)
    node = lax.broadcasted_iota(jnp.int32, (block, slots), 0) + pl.program_id(0) * block
    match = [onehot(node == idx_ref[pl.ds(peer_of(e, k), 1), :]) for _, e, k in blocks]
    match.append(onehot(node == idx_ref[len(blocks) : len(blocks) + 1, :]))
    values = [part[...] for part, _, _ in blocks] + [hub_ref[...]]
    added = mm(jnp.concatenate(match, axis=1), jnp.concatenate(values, axis=0))
    out_ref[...] = (base_ref[...] + added).astype(BF)


def finish_kernel(third_ref, self_ref, neigh_ref, bias_ref, *, factor):
    rows = third_ref.shape[0]
    share = 8
    third = third_ref[...].astype(F32)
    left = third[:, :share, :].reshape(rows * share, LANES)
    right = third[:, share : 2 * share, :].reshape(rows * share, LANES)
    grads = jnp.concatenate([left, right], axis=1) * factor
    half = grads.shape[0] // 2
    self_ref[...] = grads[:half]
    neigh_ref[...] = grads[half:]
    bias = third[0, 16:24, :]
    for r in range(1, rows):
        bias += third[r, 16:24, :]
    bias = bias[0:2] + bias[2:4]
    bias_ref[...] = jnp.concatenate([bias[0:1], bias[1:2]], axis=1) * factor


def peer_of(other_core, shift):
    me = lax.axis_index("col")
    chips = lax.axis_size("col") // 2
    return lax.rem(me // 2 + shift + chips, chips) * 2 + (me % 2 + other_core) % 2


def departures(own, other, *along):
    blocks = [(own, 0, 0), (other, 1, 0)]
    for k, part in enumerate(along):
        blocks += [(part.at[0], 0, k + 1), (part.at[1], 1, k + 1)]
    return blocks


def arrivals(own, other, *rest):
    *along, crossed = rest
    blocks = [(own, 0, 0), (other, 1, 0)]
    for k, part in enumerate(along):
        blocks += [(part.at[0], 0, -k - 1), (crossed.at[k], 1, -k - 1)]
    return blocks


def swap(parts, axis):
    return lax.all_to_all(parts, axis, split_axis=0, concat_axis=0, tiled=True)


def exchange(parts, cols):
    chips = cols // 2
    over = [(j, j ^ 1) for j in range(cols)]
    own, other, *parts = parts
    for k in range(1, chips):
        along = [(j, (j // 2 + k) % chips * 2 + j % 2) for j in range(cols)]
        parts[k - 1] = lax.ppermute(parts[k - 1], "col", along)
    other = lax.ppermute(other, "col", over)
    parts, other = lax.optimization_barrier((tuple(parts), other))
    crossed = jnp.stack([part[1] for part in parts])
    return own, other, *parts, lax.ppermute(crossed, "col", over)


def body(
    features,
    w_self,
    w_neigh,
    bias,
    cotangent,
    local_tiles,
    local_tile_idx,
    boundary_adj,
    send_rows,
    send_counts,
    hub_adj,
    hub_rows,
):
    nodes, width = features.shape
    hidden = w_self.shape[1]
    tiles, side, _ = local_tiles.shape
    peers, slots = send_rows.shape
    hub_own = hub_rows.shape[1]
    rows = lax.axis_size("row")
    cols = lax.axis_size("col")
    hubs = rows * hub_own
    received_rows = peers * slots
    struct = jax.ShapeDtypeStruct
    block = 512
    steps = nodes // block
    tile_steps = 4
    tile_block = tiles // tile_steps

    tile_index = local_tile_idx.T
    sems = lambda count: pltpu.SemaphoreType.DMA((count,))
    int32 = jnp.int32

    hub_send, *outgoing = call(
        gather_kernel,
        "gather_rows",
        (struct((rows, hub_own, width), BF),)
        + (struct((slots, width), BF),) * 2
        + (struct((2, slots, width), BF),) * (cols // 2 - 1),
        2 * (peers * slots + hub_own) * nodes * width,
        nodes * width * 2,
        vmem=60,
        in_specs=[HBM] * 4,
        scratch_shapes=[
            pltpu.SMEM((peers,), int32),
            pltpu.VMEM((peers, slots), int32),
            pltpu.VMEM((1, hub_own), int32),
            pltpu.VMEM((nodes, width), BF),
            sems(4),
        ],
    )(send_counts, send_rows, hub_rows, features)
    table = swap(hub_send, "row").reshape(hubs, width)
    received = exchange(outgoing, cols)

    share = 2 * width // rows
    depth = hub_own + 2 * share
    parcels = [struct((slots, width), BF)] * 2
    parcels += [struct((2, slots, width), BF)] * (cols // 2 - 1)

    def middle(*refs):
        outs = 10 + len(received)
        back = outs + 4
        rest = back + len(parcels)
        middle_kernel(*refs[:10], refs[10:outs], *refs[outs:back], refs[back:rest], *refs[rest:])

    grad_t, pg, first, bias_sum, *back = call(
        middle,
        "middle",
        (
            struct((width, nodes), BF),
            struct((nodes, hidden), BF),
            struct((rows, depth, width), BF),
            struct((1, hidden), F32),
            *parcels,
        ),
        8 * nodes * hubs * width,
        nodes * (hubs * 4 + width * 16),
        vmem=60,
        in_specs=[HBM] * (10 + len(received)),
        out_specs=(HBM,) * (4 + len(parcels)),
        scratch_shapes=[
            pltpu.VMEM((width, hidden), BF),
            pltpu.VMEM((width, hidden), BF),
            pltpu.VMEM((1, hidden), F32),
            pltpu.VMEM((steps, block, received_rows), BF),
            pltpu.VMEM((steps, block, hubs), BF),
            pltpu.VMEM((nodes, width), BF),
            pltpu.VMEM((steps, block, hidden), BF),
            pltpu.SMEM((2, tiles), int32),
            pltpu.VMEM((tile_steps, tile_block, side, side), BF),
            pltpu.VMEM((nodes, 2 * width), F32),
            pltpu.VMEM((received_rows, width), BF),
            pltpu.VMEM((hubs, width), BF),
            pltpu.VMEM((width, nodes), BF),
            pltpu.VMEM((steps, block, hidden), BF),
            pltpu.VMEM((rows, depth, width), BF),
            pltpu.VMEM((1, hidden), F32),
            tuple(pltpu.VMEM(part.shape, BF) for part in parcels),
            pltpu.VMEM((width, received_rows), F32),
            pltpu.VMEM((width, hubs), F32),
            pltpu.VMEM((2 * width, hidden), F32),
            sems(6 + tile_steps + 3 * steps + cols),
            sems(2 * steps + 2 + len(parcels)),
        ],
    )(
        w_self,
        w_neigh,
        bias.reshape(1, hidden),
        boundary_adj,
        hub_adj,
        features,
        cotangent,
        tile_index,
        local_tiles,
        table,
        *received,
    )
    first = swap(first, "row")

    returned = exchange(back, cols)
    first, returned = lax.optimization_barrier((first, returned))
    hub_mine, second = call(
        row_sum_kernel,
        "row_sum",
        (struct((4 * hub_own, width), BF), struct((cols, 24, width), F32)),
        rows * depth * width,
        rows * depth * width * 2,
    )(first, bias_sum)
    second = swap(second, "col")

    third = call(
        col_sum_kernel,
        "col_sum",
        struct((rows, 24, width), BF),
        cols * 24 * width,
        cols * 24 * width * 4,
    )(second)
    third, grad_t, pg = lax.optimization_barrier((third, grad_t, pg))
    third = swap(third, "row")

    base = call(
        local_back_kernel,
        "local_back",
        struct((nodes, width), F32),
        2 * tiles * side * side * width + 2 * nodes * width * hidden,
        tiles * side * side * 2 + nodes * width * 10,
        in_specs=[HBM, HBM, HBM, VMEM, VMEM],
        scratch_shapes=[
            pltpu.SMEM((2, tiles), int32),
            pltpu.VMEM((width, hidden), BF),
            pltpu.VMEM((tile_steps, tile_block, side, side), BF),
            pltpu.VMEM((nodes // side, width, side), F32),
            sems(2 + tile_steps),
        ],
    )(tile_index, w_self, local_tiles, grad_t, pg)

    slot = jnp.arange(slots, dtype=jnp.int32)[None, :]
    listed = jnp.where(slot < send_counts[:, None], send_rows, -1)
    unused = jnp.full((1, slots - 3 * hub_own), -1, jnp.int32)
    hub_slots = jnp.concatenate([hub_rows, hub_rows, hub_rows, unused], axis=1)
    index = jnp.concatenate([listed, hub_slots], axis=0)
    index = jnp.pad(index, ((0, 16 - index.shape[0]), (0, 0)), constant_values=-1)
    grad_features = call(
        scatter_kernel,
        "scatter",
        struct((nodes, width), BF),
        2 * nodes * received_rows * width,
        nodes * width * 6 + received_rows * width * 2,
        grid=(steps,),
        in_specs=[
            whole((16, slots)),
            whole((4 * hub_own, width)),
            pl.BlockSpec((block, width), lambda i: (i, 0)),
        ]
        + [whole(part.shape) for part in returned],
        out_specs=pl.BlockSpec((block, width), lambda i: (i, 0)),
    )(index, hub_mine, base, *returned)

    factor = 1.0 / math.sqrt(nodes * rows * cols)

    def finish(*refs):
        finish_kernel(*refs, factor=factor)

    grad_self, grad_neigh, grad_bias = call(
        finish,
        "finish",
        (struct((width, hidden), F32), struct((width, hidden), F32), struct((1, hidden), F32)),
        rows * 24 * width,
        rows * 24 * width * 4,
    )(third)
    return grad_features, grad_self, grad_neigh, grad_bias.reshape(hidden)


def solution(mesh):
    placed = (
        P(("row", "col"), None),
        P(),
        P(),
        P(),
        P(("row", "col"), None),
        P(("row", "col"), None, None),
        P(("row", "col"), None),
        P(("row", "col"), None),
        P(("row", "col"), None),
        P(("row", "col")),
        P(("row", "col"), None),
        P(("row", "col"), None),
    )
    return jax.shard_map(
        body,
        mesh=mesh,
        in_specs=placed,
        out_specs=(P(("row", "col"), None), P(), P(), P()),
        check_vma=False,
    )
```

```python
import math

import jax
import jax.numpy as jnp
from jax import lax
from jax.experimental import pallas as pl
from jax.experimental.pallas import tpu as pltpu
from jax.sharding import PartitionSpec as P

BF = jnp.bfloat16
F32 = jnp.float32
LANES = 128
MIB = 1 << 20


def mm(left, right):
    return jnp.dot(left, right, preferred_element_type=F32)


def with_ones(rows):
    return jnp.concatenate([rows, jnp.ones((rows.shape[0], LANES), BF)], axis=1)


def column(row):
    n = row.shape[1]
    down = lax.broadcasted_iota(jnp.int32, (n, n), 0)
    across = lax.broadcasted_iota(jnp.int32, (n, n), 1)
    picked = jnp.where(down == across, row.astype(F32), 0.0)
    return jnp.sum(picked, axis=1, keepdims=True).astype(jnp.int32)


def onehot(match):
    return jnp.where(match, 1.0, 0.0).astype(BF)


def pick_matrix(listed, nodes):
    n = listed.shape[1]
    index = column(listed)
    lanes = lax.broadcasted_iota(jnp.int32, (n, LANES), 1)
    low = onehot(lanes == (index & (LANES - 1)))
    high = jnp.broadcast_to((index >> 7).astype(F32), (n, LANES)).astype(BF)
    none = jnp.zeros((n, LANES), BF)
    parts = [jnp.where(high == jnp.asarray(b, BF), low, none) for b in range(nodes // LANES)]
    return jnp.concatenate(parts, axis=1)


def call(kernel, name, out, flops, nbytes, vmem=24, **rest):
    return pl.pallas_call(
        kernel,
        out_shape=out,
        name=name,
        cost_estimate=pl.CostEstimate(flops=flops, bytes_accessed=nbytes, transcendentals=0),
        compiler_params=pltpu.CompilerParams(vmem_limit_bytes=vmem * MIB),
        **rest,
    )


def whole(shape):
    return pl.BlockSpec(shape, lambda *_: (0,) * len(shape))


HBM = pl.BlockSpec(memory_space=pltpu.HBM)
VMEM = pl.BlockSpec(memory_space=pltpu.VMEM)


def fetch(source, target, sem):
    copy = pltpu.make_async_copy(source, target, sem)
    copy.start()
    return copy


def chunks(ref, buf, sems, first):
    size = buf.shape[1]
    return [
        fetch(ref.at[pl.ds(i * size, size)], buf.at[i], sems.at[first + i])
        for i in range(buf.shape[0])
    ]


def gather_kernel(
    counts_hbm, rows_hbm, hubs_hbm, feat_hbm, hub_ref, *rest
):
    *send_refs, counts_ref, rows_ref, hubs_ref, feat_ref, sems = rest
    copies = [
        fetch(source, target, sems.at[i])
        for i, (source, target) in enumerate(
            (
                (hubs_hbm, hubs_ref),
                (feat_hbm, feat_ref),
                (counts_hbm, counts_ref),
                (rows_hbm, rows_ref),
            )
        )
    ]
    for copy in copies:
        copy.wait()
    nodes = feat_ref.shape[0]
    slots = rows_ref.shape[1]
    slot = lax.broadcasted_iota(jnp.int32, (1, slots), 1)
    pick = pick_matrix(hubs_ref[...], nodes)
    own = mm(pick, feat_ref[...]).astype(BF)
    hub_ref[...] = jnp.broadcast_to(own[None], hub_ref.shape)
    for ref, e, k in departures(*send_refs):
        peer = peer_of(e, k)
        listed = jnp.where(slot < counts_ref[peer], rows_ref[pl.ds(peer, 1), :], -1)
        ref[...] = mm(pick_matrix(listed, nodes), feat_ref[...]).astype(BF)


def middle_kernel(
    w_self_hbm,
    w_neigh_hbm,
    bias_hbm,
    bound_hbm,
    hub_hbm,
    feat_hbm,
    cot_hbm,
    idx_hbm,
    tiles_hbm,
    table_hbm,
    parts_hbm,
    grad_t_hbm,
    pg_hbm,
    first_hbm,
    bias_sum_hbm,
    back_hbm,
    w_self_ref,
    w_neigh_ref,
    bias_ref,
    adj_ref,
    feat_ref,
    cot_ref,
    idx_ref,
    tiles_ref,
    ext_ref,
    sources_ref,
    grad_t_ref,
    pg_ref,
    first_ref,
    bias_sum,
    back_refs,
    adj_acc,
    w_acc,
    sems,
    out_sems,
):
    nodes, width = feat_ref.shape
    steps, block, _ = cot_ref.shape
    tile_steps, count, side, _ = tiles_ref.shape
    index = fetch(idx_hbm, idx_ref, sems.at[4])
    feat = fetch(feat_hbm, feat_ref, sems.at[5])
    tile_parts = chunks(tiles_hbm, tiles_ref, sems, 6)
    at_large = 6 + tile_steps
    small = [
        fetch(table_hbm, sources_ref.at[pl.ds(bound_hbm.shape[1], hub_hbm.shape[1])], sems.at[3]),
        fetch(w_self_hbm, w_self_ref, sems.at[0]),
        fetch(w_neigh_hbm, w_neigh_ref, sems.at[1]),
        fetch(bias_hbm, bias_ref, sems.at[2]),
    ]
    slots = parts_hbm[0].shape[0]
    for n, (source, e, k) in enumerate(arrivals(*parts_hbm)):
        to = sources_ref.at[pl.ds(pl.multiple_of(peer_of(e, k) * slots, slots), slots)]
        small.append(fetch(source, to, sems.at[at_large + 3 * steps + n]))
    width_in = bound_hbm.shape[1]
    pairs = (
        (bound_hbm, adj_ref, (slice(None), pl.ds(0, width_in))),
        (hub_hbm, adj_ref, (slice(None), pl.ds(width_in, hub_hbm.shape[1]))),
        (cot_hbm, cot_ref, ()),
    )
    large = []
    for i in range(steps):
        rows = pl.ds(i * block, block)
        large.append(
            [
                fetch(source.at[rows], target.at[(i, *part)], sems.at[at_large + 3 * i + j])
                for j, (source, target, part) in enumerate(pairs)
            ]
        )
    ext_ref[...] = jnp.zeros_like(ext_ref)
    index.wait()
    feat.wait()
    for step in range(tile_steps):
        tile_parts[step].wait()
        for t in range(count):
            k = step * count + t
            to = pl.multiple_of(idx_ref[0, k] * side, side)
            at = pl.multiple_of(idx_ref[1, k] * side, side)
            rows = with_ones(feat_ref[pl.ds(at, side), :])
            ext_ref[pl.ds(to, side), :] += mm(tiles_ref[step, t], rows)
    for copy in small:
        copy.wait()
    sources = with_ones(sources_ref[...])
    w_both = jnp.concatenate([w_self_ref[...], w_neigh_ref[...]], axis=0)
    stores = []
    summed, done = {}, {}
    for i in range(steps + 2):
        if i < steps:
            for copy in large[i]:
                copy.wait()
            rows = pl.ds(i * block, block)
            summed[i] = ext_ref[rows, :] + mm(adj_ref[i], sources)
        if 0 <= i - 1 < steps:
            c = i - 1
            rows = pl.ds(c * block, block)
            ext = summed.pop(c)
            inverse = 1.0 / (1.0 + ext[:, width:])
            mean = (ext[:, :width] * inverse).astype(BF)
            both = jnp.concatenate([feat_ref[rows, :], mean], axis=1)
            preact = mm(both, w_both) + bias_ref[...]
            slope = jnp.where(preact > 0, 1.0, jnp.exp(jnp.minimum(preact, 0.0)))
            pg = (cot_ref[c].astype(F32) * slope).astype(BF)
            pg_ref[c] = pg
            grad = lax.dot_general(
                pg, w_neigh_ref[...], (((1,), (1,)), ((), ())), preferred_element_type=F32
            )
            grad_t = jnp.transpose(grad * inverse).astype(BF)
            grad_t_ref[:, rows] = grad_t
            done[c] = (both, pg, grad_t)
        if 0 <= i - 2 < steps:
            c = i - 2
            last_both, last_pg, last_grad_t = done.pop(c)
            adj_part = mm(last_grad_t, adj_ref[c])
            w_part = mm(jnp.transpose(last_both), last_pg)
            bias_part = jnp.sum(last_pg.astype(F32), axis=0, keepdims=True)
            if c == 0:
                adj_acc[...] = adj_part
                w_acc[...] = w_part
                bias_sum[...] = bias_part
            else:
                adj_acc[...] += adj_part
                w_acc[...] += w_part
                bias_sum[...] += bias_part
        if 0 <= i - 1 < steps:
            c = i - 1
            rows = pl.ds(c * block, block)
            stores.append(fetch(pg_ref.at[c], pg_hbm.at[rows], out_sems.at[2 * c]))
            stores.append(
                fetch(grad_t_ref.at[:, rows], grad_t_hbm.at[:, rows], out_sems.at[2 * c + 1])
            )
    rows, depth, _ = first_ref.shape
    hubs = hub_hbm.shape[1] // rows
    share = w_acc.shape[0] // rows
    hub_back = jnp.transpose(adj_acc[:, width_in:]).astype(BF)
    first_ref[:, :hubs, :] = hub_back.reshape(rows, hubs, width)
    left = w_acc[:, :LANES].reshape(rows, share, LANES)
    right = w_acc[:, LANES:].reshape(rows, share, LANES)
    first_ref[:, hubs:, :] = jnp.concatenate([left, right], axis=1).astype(BF)
    stores.append(fetch(first_ref, first_hbm, out_sems.at[2 * steps]))
    stores.append(fetch(bias_sum, bias_sum_hbm, out_sems.at[2 * steps + 1]))
    for ref, e, k in departures(*back_refs):
        at = pl.multiple_of(peer_of(e, k) * LANES, LANES)
        ref[...] = jnp.transpose(adj_acc[:, pl.ds(at, LANES)]).astype(BF)
    for n, (source, target) in enumerate(zip(back_refs, back_hbm)):
        stores.append(fetch(source, target, out_sems.at[2 * steps + 2 + n]))
    for store in stores:
        store.wait()


def local_back_kernel(
    idx_hbm,
    w_self_hbm,
    tiles_hbm,
    grad_t_ref,
    pg_ref,
    out_ref,
    idx_ref,
    w_self_ref,
    tiles_ref,
    acc,
    sems,
):
    index = fetch(idx_hbm, idx_ref, sems.at[0])
    weights = fetch(w_self_hbm, w_self_ref, sems.at[1])
    parts = chunks(tiles_hbm, tiles_ref, sems, 2)
    acc[...] = jnp.zeros_like(acc)
    steps, count, side, _ = tiles_ref.shape
    index.wait()
    weights.wait()
    for step in range(steps):
        parts[step].wait()
        for t in range(count):
            k = step * count + t
            at = pl.multiple_of(idx_ref[0, k] * side, side)
            acc[idx_ref[1, k]] += mm(grad_t_ref[:, pl.ds(at, side)], tiles_ref[step, t])
    for b in range(acc.shape[0]):
        rows = pl.ds(b * side, side)
        own = lax.dot_general(
            pg_ref[rows, :],
            w_self_ref[...],
            (((1,), (1,)), ((), ())),
            preferred_element_type=F32,
        )
        out_ref[rows, :] = own + jnp.transpose(acc[b])


def row_sum_kernel(first_ref, bias_ref, hub_ref, second_ref):
    rows, depth, width = first_ref.shape
    total = first_ref[0].astype(F32)
    for r in range(1, rows):
        total += first_ref[r].astype(F32)
    hubs = depth - 16
    hub = total[:hubs]
    high = hub.astype(BF)
    rest = hub - high.astype(F32)
    middle = rest.astype(BF)
    low = (rest - middle.astype(F32)).astype(BF)
    hub_ref[...] = jnp.concatenate([high, middle, low, jnp.zeros((hubs, width), BF)], axis=0)
    mine = jnp.concatenate([total[hubs:], bias_ref[...]], axis=0)
    second_ref[...] = jnp.broadcast_to(mine[None], second_ref.shape)


def col_sum_kernel(second_ref, third_ref):
    total = second_ref[0]
    for p in range(1, second_ref.shape[0]):
        total += second_ref[p]
    bias = total[16:18]
    rest = bias - bias.astype(BF).astype(F32)
    done = jnp.concatenate([total[:18], rest, total[20:]], axis=0).astype(BF)
    third_ref[...] = jnp.broadcast_to(done[None], third_ref.shape)


def scatter_kernel(idx_ref, hub_ref, base_ref, *refs):
    *parts, out_ref = refs
    block = out_ref.shape[0]
    slots = idx_ref.shape[1]
    blocks = arrivals(*parts)
    node = lax.broadcasted_iota(jnp.int32, (block, slots), 0) + pl.program_id(0) * block
    match = [onehot(node == idx_ref[pl.ds(peer_of(e, k), 1), :]) for _, e, k in blocks]
    match.append(onehot(node == idx_ref[len(blocks) : len(blocks) + 1, :]))
    values = [part[...] for part, _, _ in blocks] + [hub_ref[...]]
    added = mm(jnp.concatenate(match, axis=1), jnp.concatenate(values, axis=0))
    out_ref[...] = (base_ref[...] + added).astype(BF)


def finish_kernel(third_ref, self_ref, neigh_ref, bias_ref, *, factor):
    rows = third_ref.shape[0]
    share = 8
    third = third_ref[...].astype(F32)
    left = third[:, :share, :].reshape(rows * share, LANES)
    right = third[:, share : 2 * share, :].reshape(rows * share, LANES)
    grads = jnp.concatenate([left, right], axis=1) * factor
    half = grads.shape[0] // 2
    self_ref[...] = grads[:half]
    neigh_ref[...] = grads[half:]
    bias = third[0, 16:24, :]
    for r in range(1, rows):
        bias += third[r, 16:24, :]
    bias = bias[0:2] + bias[2:4]
    bias_ref[...] = jnp.concatenate([bias[0:1], bias[1:2]], axis=1) * factor


def peer_of(other_core, shift):
    me = lax.axis_index("col")
    chips = lax.axis_size("col") // 2
    return lax.rem(me // 2 + shift + chips, chips) * 2 + (me % 2 + other_core) % 2


def departures(own, other, *along):
    blocks = [(own, 0, 0), (other, 1, 0)]
    for k, part in enumerate(along):
        blocks += [(part.at[0], 0, k + 1), (part.at[1], 1, k + 1)]
    return blocks


def arrivals(own, other, *rest):
    *along, crossed = rest
    blocks = [(own, 0, 0), (other, 1, 0)]
    for k, part in enumerate(along):
        blocks += [(part.at[0], 0, -k - 1), (crossed.at[k], 1, -k - 1)]
    return blocks


def swap(parts, axis):
    return lax.all_to_all(parts, axis, split_axis=0, concat_axis=0, tiled=True)


def exchange(parts, cols):
    chips = cols // 2
    over = [(j, j ^ 1) for j in range(cols)]
    own, other, *parts = parts
    for k in range(1, chips):
        along = [(j, (j // 2 + k) % chips * 2 + j % 2) for j in range(cols)]
        parts[k - 1] = lax.ppermute(parts[k - 1], "col", along)
    other = lax.ppermute(other, "col", over)
    parts, other = lax.optimization_barrier((tuple(parts), other))
    crossed = jnp.stack([part[1] for part in parts])
    return own, other, *parts, lax.ppermute(crossed, "col", over)


def body(
    features,
    w_self,
    w_neigh,
    bias,
    cotangent,
    local_tiles,
    local_tile_idx,
    boundary_adj,
    send_rows,
    send_counts,
    hub_adj,
    hub_rows,
):
    nodes, width = features.shape
    hidden = w_self.shape[1]
    tiles, side, _ = local_tiles.shape
    peers, slots = send_rows.shape
    hub_own = hub_rows.shape[1]
    rows = lax.axis_size("row")
    cols = lax.axis_size("col")
    hubs = rows * hub_own
    received_rows = peers * slots
    struct = jax.ShapeDtypeStruct
    block = 512
    steps = nodes // block
    tile_steps = 4
    tile_block = tiles // tile_steps

    tile_index = local_tile_idx.T
    sems = lambda count: pltpu.SemaphoreType.DMA((count,))
    int32 = jnp.int32

    hub_send, *outgoing = call(
        gather_kernel,
        "gather_rows",
        (struct((rows, hub_own, width), BF),)
        + (struct((slots, width), BF),) * 2
        + (struct((2, slots, width), BF),) * (cols // 2 - 1),
        2 * (peers * slots + hub_own) * nodes * width,
        nodes * width * 2,
        vmem=60,
        in_specs=[HBM] * 4,
        scratch_shapes=[
            pltpu.SMEM((peers,), int32),
            pltpu.VMEM((peers, slots), int32),
            pltpu.VMEM((1, hub_own), int32),
            pltpu.VMEM((nodes, width), BF),
            sems(4),
        ],
    )(send_counts, send_rows, hub_rows, features)
    table = swap(hub_send, "row").reshape(hubs, width)
    received = exchange(outgoing, cols)

    share = 2 * width // rows
    block, steps = 1024, nodes // 1024
    depth = hub_own + 2 * share
    parcels = [struct((slots, width), BF)] * 2
    parcels += [struct((2, slots, width), BF)] * (cols // 2 - 1)

    def middle(*refs):
        outs = 10 + len(received)
        back = outs + 4
        rest = back + len(parcels)
        middle_kernel(*refs[:10], refs[10:outs], *refs[outs:back], refs[back:rest], *refs[rest:])

    grad_t, pg, first, bias_sum, *back = call(
        middle,
        "middle",
        (
            struct((width, nodes), BF),
            struct((nodes, hidden), BF),
            struct((rows, depth, width), BF),
            struct((1, hidden), F32),
            *parcels,
        ),
        8 * nodes * hubs * width,
        nodes * (hubs * 4 + width * 16),
        vmem=60,
        in_specs=[HBM] * (10 + len(received)),
        out_specs=(HBM,) * (4 + len(parcels)),
        scratch_shapes=[
            pltpu.VMEM((width, hidden), BF),
            pltpu.VMEM((width, hidden), BF),
            pltpu.VMEM((1, hidden), F32),
            pltpu.VMEM((steps, block, received_rows + hubs), BF),
            pltpu.VMEM((nodes, width), BF),
            pltpu.VMEM((steps, block, hidden), BF),
            pltpu.SMEM((2, tiles), int32),
            pltpu.VMEM((tile_steps, tile_block, side, side), BF),
            pltpu.VMEM((nodes, 2 * width), F32),
            pltpu.VMEM((received_rows + hubs, width), BF),
            pltpu.VMEM((width, nodes), BF),
            pltpu.VMEM((steps, block, hidden), BF),
            pltpu.VMEM((rows, depth, width), BF),
            pltpu.VMEM((1, hidden), F32),
            tuple(pltpu.VMEM(part.shape, BF) for part in parcels),
            pltpu.VMEM((width, received_rows + hubs), F32),
            pltpu.VMEM((2 * width, hidden), F32),
            sems(6 + tile_steps + 3 * steps + cols),
            sems(2 * steps + 2 + len(parcels)),
        ],
    )(
        w_self,
        w_neigh,
        bias.reshape(1, hidden),
        boundary_adj,
        hub_adj,
        features,
        cotangent,
        tile_index,
        local_tiles,
        table,
        *received,
    )
    first = swap(first, "row")

    block, steps = 512, nodes // 512
    returned = exchange(back, cols)
    bias_rows = jnp.pad(bias_sum.reshape(-1, width), ((0, 8 - hidden // width), (0, 0)))
    first, returned, bias_rows = lax.optimization_barrier((first, returned, bias_rows))
    hub_mine, second = call(
        row_sum_kernel,
        "row_sum",
        (struct((4 * hub_own, width), BF), struct((cols, 24, width), F32)),
        rows * depth * width,
        rows * depth * width * 2,
    )(first, bias_rows)
    second = swap(second, "col")

    third = call(
        col_sum_kernel,
        "col_sum",
        struct((rows, 24, width), BF),
        cols * 24 * width,
        cols * 24 * width * 4,
    )(second)
    third, grad_t, pg = lax.optimization_barrier((third, grad_t, pg))
    third = swap(third, "row")

    base = call(
        local_back_kernel,
        "local_back",
        struct((nodes, width), F32),
        2 * tiles * side * side * width + 2 * nodes * width * hidden,
        tiles * side * side * 2 + nodes * width * 10,
        in_specs=[HBM, HBM, HBM, VMEM, VMEM],
        scratch_shapes=[
            pltpu.SMEM((2, tiles), int32),
            pltpu.VMEM((width, hidden), BF),
            pltpu.VMEM((tile_steps, tile_block, side, side), BF),
            pltpu.VMEM((nodes // side, width, side), F32),
            sems(2 + tile_steps),
        ],
    )(tile_index, w_self, local_tiles, grad_t, pg)

    slot = jnp.arange(slots, dtype=jnp.int32)[None, :]
    listed = jnp.where(slot < send_counts[:, None], send_rows, -1)
    unused = jnp.full((1, slots - 3 * hub_own), -1, jnp.int32)
    hub_slots = jnp.concatenate([hub_rows, hub_rows, hub_rows, unused], axis=1)
    index = jnp.concatenate([listed, hub_slots], axis=0)
    index = jnp.pad(index, ((0, 16 - index.shape[0]), (0, 0)), constant_values=-1)
    grad_features = call(
        scatter_kernel,
        "scatter",
        struct((nodes, width), BF),
        2 * nodes * received_rows * width,
        nodes * width * 6 + received_rows * width * 2,
        grid=(steps,),
        in_specs=[
            whole((16, slots)),
            whole((4 * hub_own, width)),
            pl.BlockSpec((block, width), lambda i: (i, 0)),
        ]
        + [whole(part.shape) for part in returned],
        out_specs=pl.BlockSpec((block, width), lambda i: (i, 0)),
    )(index, hub_mine, base, *returned)

    factor = 1.0 / math.sqrt(nodes * rows * cols)

    def finish(*refs):
        finish_kernel(*refs, factor=factor)

    grad_self, grad_neigh, grad_bias = call(
        finish,
        "finish",
        (struct((width, hidden), F32), struct((width, hidden), F32), struct((1, hidden), F32)),
        rows * 24 * width,
        rows * 24 * width * 4,
    )(third)
    return grad_features, grad_self, grad_neigh, grad_bias.reshape(hidden)


def solution(mesh):
    placed = (
        P(("row", "col"), None),
        P(),
        P(),
        P(),
        P(("row", "col"), None),
        P(("row", "col"), None, None),
        P(("row", "col"), None),
        P(("row", "col"), None),
        P(("row", "col"), None),
        P(("row", "col")),
        P(("row", "col"), None),
        P(("row", "col"), None),
    )
    return jax.shard_map(
        body,
        mesh=mesh,
        in_specs=placed,
        out_specs=(P(("row", "col"), None), P(), P(), P()),
        check_vma=False,
    )
```

```python
import math

import jax
import jax.numpy as jnp
from jax import lax
from jax.experimental import pallas as pl
from jax.experimental.pallas import tpu as pltpu
from jax.sharding import PartitionSpec as P

BF = jnp.bfloat16
F32 = jnp.float32
LANES = 128
MIB = 1 << 20


def mm(left, right):
    return jnp.dot(left, right, preferred_element_type=F32)


def with_ones(rows):
    return jnp.concatenate([rows, jnp.ones((rows.shape[0], LANES), BF)], axis=1)


def column(row):
    n = row.shape[1]
    down = lax.broadcasted_iota(jnp.int32, (n, n), 0)
    across = lax.broadcasted_iota(jnp.int32, (n, n), 1)
    picked = jnp.where(down == across, row.astype(F32), 0.0)
    return jnp.sum(picked, axis=1, keepdims=True).astype(jnp.int32)


def onehot(match):
    return jnp.where(match, 1.0, 0.0).astype(BF)


def pick_matrix(listed, nodes):
    n = listed.shape[1]
    index = column(listed)
    lanes = lax.broadcasted_iota(jnp.int32, (n, LANES), 1)
    low = onehot(lanes == (index & (LANES - 1)))
    high = jnp.broadcast_to((index >> 7).astype(F32), (n, LANES)).astype(BF)
    none = jnp.zeros((n, LANES), BF)
    parts = [jnp.where(high == jnp.asarray(b, BF), low, none) for b in range(nodes // LANES)]
    return jnp.concatenate(parts, axis=1)


def call(kernel, name, out, flops, nbytes, vmem=24, **rest):
    return pl.pallas_call(
        kernel,
        out_shape=out,
        name=name,
        cost_estimate=pl.CostEstimate(flops=flops, bytes_accessed=nbytes, transcendentals=0),
        compiler_params=pltpu.CompilerParams(vmem_limit_bytes=vmem * MIB),
        **rest,
    )


def whole(shape):
    return pl.BlockSpec(shape, lambda *_: (0,) * len(shape))


HBM = pl.BlockSpec(memory_space=pltpu.HBM)
VMEM = pl.BlockSpec(memory_space=pltpu.VMEM)


def fetch(source, target, sem):
    copy = pltpu.make_async_copy(source, target, sem)
    copy.start()
    return copy


def chunks(ref, buf, sems, first):
    size = buf.shape[1]
    return [
        fetch(ref.at[pl.ds(i * size, size)], buf.at[i], sems.at[first + i])
        for i in range(buf.shape[0])
    ]


def gather_kernel(
    counts_hbm, rows_hbm, hubs_hbm, feat_hbm, hub_ref, *rest
):
    *send_refs, counts_ref, rows_ref, hubs_ref, feat_ref, sems = rest
    copies = [
        fetch(source, target, sems.at[i])
        for i, (source, target) in enumerate(
            (
                (hubs_hbm, hubs_ref),
                (feat_hbm, feat_ref),
                (counts_hbm, counts_ref),
                (rows_hbm, rows_ref),
            )
        )
    ]
    for copy in copies:
        copy.wait()
    nodes = feat_ref.shape[0]
    slots = rows_ref.shape[1]
    slot = lax.broadcasted_iota(jnp.int32, (1, slots), 1)
    pick = pick_matrix(hubs_ref[...], nodes)
    own = mm(pick, feat_ref[...]).astype(BF)
    hub_ref[...] = jnp.broadcast_to(own[None], hub_ref.shape)
    for ref, e, k in departures(*send_refs):
        peer = peer_of(e, k)
        listed = jnp.where(slot < counts_ref[peer], rows_ref[pl.ds(peer, 1), :], -1)
        ref[...] = mm(pick_matrix(listed, nodes), feat_ref[...]).astype(BF)


def middle_kernel(
    w_self_hbm,
    w_neigh_hbm,
    bias_hbm,
    bound_hbm,
    hub_hbm,
    feat_hbm,
    cot_hbm,
    idx_hbm,
    tiles_hbm,
    table_hbm,
    parts_hbm,
    grad_t_hbm,
    pg_hbm,
    first_hbm,
    bias_sum_hbm,
    back_hbm,
    w_self_ref,
    w_neigh_ref,
    bias_ref,
    adj_ref,
    feat_ref,
    cot_ref,
    idx_ref,
    tiles_ref,
    ext_ref,
    sources_ref,
    grad_t_ref,
    pg_ref,
    first_ref,
    bias_sum,
    back_refs,
    adj_acc,
    w_acc,
    sems,
    out_sems,
):
    nodes, width = feat_ref.shape
    steps, block, _ = cot_ref.shape
    tile_steps, count, side, _ = tiles_ref.shape
    index = fetch(idx_hbm, idx_ref, sems.at[4])
    feat = fetch(feat_hbm, feat_ref, sems.at[5])
    tile_parts = chunks(tiles_hbm, tiles_ref, sems, 6)
    at_large = 6 + tile_steps
    small = [
        fetch(table_hbm, sources_ref.at[pl.ds(bound_hbm.shape[1], hub_hbm.shape[1])], sems.at[3]),
        fetch(w_self_hbm, w_self_ref, sems.at[0]),
        fetch(w_neigh_hbm, w_neigh_ref, sems.at[1]),
        fetch(bias_hbm, bias_ref, sems.at[2]),
    ]
    slots = parts_hbm[0].shape[0]
    for n, (source, e, k) in enumerate(arrivals(*parts_hbm)):
        to = sources_ref.at[pl.ds(pl.multiple_of(peer_of(e, k) * slots, slots), slots)]
        small.append(fetch(source, to, sems.at[at_large + 3 * steps + n]))
    width_in = bound_hbm.shape[1]
    pairs = (
        (bound_hbm, adj_ref, (slice(None), pl.ds(0, width_in))),
        (hub_hbm, adj_ref, (slice(None), pl.ds(width_in, hub_hbm.shape[1]))),
        (cot_hbm, cot_ref, ()),
    )
    large = []
    for i in range(steps):
        rows = pl.ds(i * block, block)
        large.append(
            [
                fetch(source.at[rows], target.at[(i, *part)], sems.at[at_large + 3 * i + j])
                for j, (source, target, part) in enumerate(pairs)
            ]
        )
    ext_ref[...] = jnp.zeros_like(ext_ref)
    index.wait()
    feat.wait()
    for step in range(tile_steps):
        tile_parts[step].wait()
        for t in range(count):
            k = step * count + t
            to = pl.multiple_of(idx_ref[0, k] * side, side)
            at = pl.multiple_of(idx_ref[1, k] * side, side)
            rows = with_ones(feat_ref[pl.ds(at, side), :])
            ext_ref[pl.ds(to, side), :] += mm(tiles_ref[step, t], rows)
    for copy in small:
        copy.wait()
    sources = with_ones(sources_ref[...])
    w_both = jnp.concatenate([w_self_ref[...], w_neigh_ref[...]], axis=0)
    stores = []
    summed, done = {}, {}
    for i in range(steps + 2):
        if i < steps:
            for copy in large[i]:
                copy.wait()
            rows = pl.ds(i * block, block)
            summed[i] = ext_ref[rows, :] + mm(adj_ref[i], sources)
        if 0 <= i - 1 < steps:
            c = i - 1
            rows = pl.ds(c * block, block)
            ext = summed.pop(c)
            inverse = 1.0 / (1.0 + ext[:, width:])
            mean = (ext[:, :width] * inverse).astype(BF)
            both = jnp.concatenate([feat_ref[rows, :], mean], axis=1)
            preact = mm(both, w_both) + bias_ref[...]
            slope = jnp.where(preact > 0, 1.0, jnp.exp(jnp.minimum(preact, 0.0)))
            pg = (cot_ref[c].astype(F32) * slope).astype(BF)
            pg_ref[c] = pg
            grad = lax.dot_general(
                pg, w_neigh_ref[...], (((1,), (1,)), ((), ())), preferred_element_type=F32
            )
            grad_t = jnp.transpose(grad * inverse).astype(BF)
            grad_t_ref[:, rows] = grad_t
            done[c] = (both, pg, grad_t)
        if 0 <= i - 2 < steps:
            c = i - 2
            last_both, last_pg, last_grad_t = done.pop(c)
            adj_part = mm(last_grad_t, adj_ref[c])
            w_part = lax.dot_general(
                last_both, last_pg, (((0,), (0,)), ((), ())), preferred_element_type=F32
            )
            bias_part = jnp.sum(last_pg.astype(F32), axis=0, keepdims=True)
            if c == 0:
                adj_acc[...] = adj_part
                w_acc[...] = w_part
                bias_sum[...] = bias_part
            else:
                adj_acc[...] += adj_part
                w_acc[...] += w_part
                bias_sum[...] += bias_part
        if 0 <= i - 1 < steps:
            c = i - 1
            rows = pl.ds(c * block, block)
            stores.append(fetch(pg_ref.at[c], pg_hbm.at[rows], out_sems.at[2 * c]))
            stores.append(
                fetch(grad_t_ref.at[:, rows], grad_t_hbm.at[:, rows], out_sems.at[2 * c + 1])
            )
    rows, depth, _ = first_ref.shape
    hubs = hub_hbm.shape[1] // rows
    share = w_acc.shape[0] // rows
    hub_back = jnp.transpose(adj_acc[:, width_in:]).astype(BF)
    first_ref[:, :hubs, :] = hub_back.reshape(rows, hubs, width)
    left = w_acc[:, :LANES].reshape(rows, share, LANES)
    right = w_acc[:, LANES:].reshape(rows, share, LANES)
    first_ref[:, hubs:, :] = jnp.concatenate([left, right], axis=1).astype(BF)
    stores.append(fetch(first_ref, first_hbm, out_sems.at[2 * steps]))
    stores.append(fetch(bias_sum, bias_sum_hbm, out_sems.at[2 * steps + 1]))
    for ref, e, k in departures(*back_refs):
        at = pl.multiple_of(peer_of(e, k) * LANES, LANES)
        ref[...] = jnp.transpose(adj_acc[:, pl.ds(at, LANES)]).astype(BF)
    for n, (source, target) in enumerate(zip(back_refs, back_hbm)):
        stores.append(fetch(source, target, out_sems.at[2 * steps + 2 + n]))
    for store in stores:
        store.wait()


def local_back_kernel(
    idx_hbm,
    w_self_hbm,
    tiles_hbm,
    grad_t_ref,
    pg_ref,
    out_ref,
    idx_ref,
    w_self_ref,
    tiles_ref,
    acc,
    sems,
):
    index = fetch(idx_hbm, idx_ref, sems.at[0])
    weights = fetch(w_self_hbm, w_self_ref, sems.at[1])
    parts = chunks(tiles_hbm, tiles_ref, sems, 2)
    acc[...] = jnp.zeros_like(acc)
    steps, count, side, _ = tiles_ref.shape
    index.wait()
    weights.wait()
    for step in range(steps):
        parts[step].wait()
        for t in range(count):
            k = step * count + t
            at = pl.multiple_of(idx_ref[0, k] * side, side)
            acc[idx_ref[1, k]] += mm(grad_t_ref[:, pl.ds(at, side)], tiles_ref[step, t])
    for b in range(acc.shape[0]):
        rows = pl.ds(b * side, side)
        own = lax.dot_general(
            pg_ref[rows, :],
            w_self_ref[...],
            (((1,), (1,)), ((), ())),
            preferred_element_type=F32,
        )
        out_ref[rows, :] = own + jnp.transpose(acc[b])


def row_sum_kernel(first_ref, bias_ref, hub_ref, second_ref):
    rows, depth, width = first_ref.shape
    total = first_ref[0].astype(F32)
    for r in range(1, rows):
        total += first_ref[r].astype(F32)
    hubs = depth - 16
    hub = total[:hubs]
    high = hub.astype(BF)
    rest = hub - high.astype(F32)
    middle = rest.astype(BF)
    low = (rest - middle.astype(F32)).astype(BF)
    hub_ref[...] = jnp.concatenate([high, middle, low, jnp.zeros((hubs, width), BF)], axis=0)
    mine = jnp.concatenate([total[hubs:], bias_ref[...]], axis=0)
    second_ref[...] = jnp.broadcast_to(mine[None], second_ref.shape)


def col_sum_kernel(second_ref, third_ref):
    total = second_ref[0]
    for p in range(1, second_ref.shape[0]):
        total += second_ref[p]
    bias = total[16:18]
    rest = bias - bias.astype(BF).astype(F32)
    none = jnp.zeros((third_ref.shape[1] - 20, total.shape[1]), F32)
    done = jnp.concatenate([total[:18], rest, none], axis=0).astype(BF)
    third_ref[...] = jnp.broadcast_to(done[None], third_ref.shape)


def scatter_kernel(idx_ref, hub_ref, base_ref, *refs):
    *parts, out_ref = refs
    block = out_ref.shape[0]
    slots = idx_ref.shape[1]
    blocks = arrivals(*parts)
    node = lax.broadcasted_iota(jnp.int32, (block, slots), 0) + pl.program_id(0) * block
    match = [onehot(node == idx_ref[pl.ds(peer_of(e, k), 1), :]) for _, e, k in blocks]
    match.append(onehot(node == idx_ref[len(blocks) : len(blocks) + 1, :]))
    values = [part[...] for part, _, _ in blocks] + [hub_ref[...]]
    added = mm(jnp.concatenate(match, axis=1), jnp.concatenate(values, axis=0))
    out_ref[...] = (base_ref[...] + added).astype(BF)


def finish_kernel(third_ref, self_ref, neigh_ref, bias_ref, *, factor):
    rows = third_ref.shape[0]
    share = 8
    third = third_ref[...].astype(F32)
    left = third[:, :share, :].reshape(rows * share, LANES)
    right = third[:, share : 2 * share, :].reshape(rows * share, LANES)
    grads = jnp.concatenate([left, right], axis=1) * factor
    half = grads.shape[0] // 2
    self_ref[...] = grads[:half]
    neigh_ref[...] = grads[half:]
    bias = third[0, 16:24, :]
    for r in range(1, rows):
        bias += third[r, 16:24, :]
    bias = bias[0:2] + bias[2:4]
    bias_ref[...] = jnp.concatenate([bias[0:1], bias[1:2]], axis=1) * factor


def peer_of(other_core, shift):
    me = lax.axis_index("col")
    chips = lax.axis_size("col") // 2
    return lax.rem(me // 2 + shift + chips, chips) * 2 + (me % 2 + other_core) % 2


def departures(own, other, *along):
    blocks = [(own, 0, 0), (other, 1, 0)]
    for k, part in enumerate(along):
        blocks += [(part.at[0], 0, k + 1), (part.at[1], 1, k + 1)]
    return blocks


def arrivals(own, other, *rest):
    *along, crossed = rest
    blocks = [(own, 0, 0), (other, 1, 0)]
    for k, part in enumerate(along):
        blocks += [(part.at[0], 0, -k - 1), (crossed.at[k], 1, -k - 1)]
    return blocks


def swap(parts, axis):
    return lax.all_to_all(parts, axis, split_axis=0, concat_axis=0, tiled=True)


def exchange(parts, cols):
    chips = cols // 2
    over = [(j, j ^ 1) for j in range(cols)]
    own, other, *parts = parts
    for k in range(1, chips):
        along = [(j, (j // 2 + k) % chips * 2 + j % 2) for j in range(cols)]
        parts[k - 1] = lax.ppermute(parts[k - 1], "col", along)
    other = lax.ppermute(other, "col", over)
    parts, other = lax.optimization_barrier((tuple(parts), other))
    crossed = jnp.stack([part[1] for part in parts])
    return own, other, *parts, lax.ppermute(crossed, "col", over)


def body(
    features,
    w_self,
    w_neigh,
    bias,
    cotangent,
    local_tiles,
    local_tile_idx,
    boundary_adj,
    send_rows,
    send_counts,
    hub_adj,
    hub_rows,
):
    nodes, width = features.shape
    hidden = w_self.shape[1]
    tiles, side, _ = local_tiles.shape
    peers, slots = send_rows.shape
    hub_own = hub_rows.shape[1]
    rows = lax.axis_size("row")
    cols = lax.axis_size("col")
    hubs = rows * hub_own
    received_rows = peers * slots
    struct = jax.ShapeDtypeStruct
    block = 512
    steps = nodes // block
    tile_steps = 4
    tile_block = tiles // tile_steps

    tile_index = local_tile_idx.T
    sems = lambda count: pltpu.SemaphoreType.DMA((count,))
    int32 = jnp.int32

    hub_send, *outgoing = call(
        gather_kernel,
        "gather_rows",
        (struct((rows, hub_own, width), BF),)
        + (struct((slots, width), BF),) * 2
        + (struct((2, slots, width), BF),) * (cols // 2 - 1),
        2 * (peers * slots + hub_own) * nodes * width,
        nodes * width * 2,
        vmem=60,
        in_specs=[HBM] * 4,
        scratch_shapes=[
            pltpu.SMEM((peers,), int32),
            pltpu.VMEM((peers, slots), int32),
            pltpu.VMEM((1, hub_own), int32),
            pltpu.VMEM((nodes, width), BF),
            sems(4),
        ],
    )(send_counts, send_rows, hub_rows, features)
    table = swap(hub_send, "row").reshape(hubs, width)
    received = exchange(outgoing, cols)

    share = 2 * width // rows
    block, steps = 1024, nodes // 1024
    depth = hub_own + 2 * share
    parcels = [struct((slots, width), BF)] * 2
    parcels += [struct((2, slots, width), BF)] * (cols // 2 - 1)

    def middle(*refs):
        outs = 10 + len(received)
        back = outs + 4
        rest = back + len(parcels)
        middle_kernel(*refs[:10], refs[10:outs], *refs[outs:back], refs[back:rest], *refs[rest:])

    grad_t, pg, first, bias_sum, *back = call(
        middle,
        "middle",
        (
            struct((width, nodes), BF),
            struct((nodes, hidden), BF),
            struct((rows, depth, width), BF),
            struct((1, hidden), F32),
            *parcels,
        ),
        8 * nodes * hubs * width,
        nodes * (hubs * 4 + width * 16),
        vmem=60,
        in_specs=[HBM] * (10 + len(received)),
        out_specs=(HBM,) * (4 + len(parcels)),
        scratch_shapes=[
            pltpu.VMEM((width, hidden), BF),
            pltpu.VMEM((width, hidden), BF),
            pltpu.VMEM((1, hidden), F32),
            pltpu.VMEM((steps, block, received_rows + hubs), BF),
            pltpu.VMEM((nodes, width), BF),
            pltpu.VMEM((steps, block, hidden), BF),
            pltpu.SMEM((2, tiles), int32),
            pltpu.VMEM((tile_steps, tile_block, side, side), BF),
            pltpu.VMEM((nodes, 2 * width), F32),
            pltpu.VMEM((received_rows + hubs, width), BF),
            pltpu.VMEM((width, nodes), BF),
            pltpu.VMEM((steps, block, hidden), BF),
            pltpu.VMEM((rows, depth, width), BF),
            pltpu.VMEM((1, hidden), F32),
            tuple(pltpu.VMEM(part.shape, BF) for part in parcels),
            pltpu.VMEM((width, received_rows + hubs), F32),
            pltpu.VMEM((2 * width, hidden), F32),
            sems(6 + tile_steps + 3 * steps + cols),
            sems(2 * steps + 2 + len(parcels)),
        ],
    )(
        w_self,
        w_neigh,
        bias.reshape(1, hidden),
        boundary_adj,
        hub_adj,
        features,
        cotangent,
        tile_index,
        local_tiles,
        table,
        *received,
    )
    first = swap(first, "row")

    block, steps = 512, nodes // 512
    returned = exchange(back, cols)
    bias_rows = jnp.pad(bias_sum.reshape(-1, width), ((0, 8 - hidden // width), (0, 0)))
    first, returned, bias_rows = lax.optimization_barrier((first, returned, bias_rows))
    hub_mine, second = call(
        row_sum_kernel,
        "row_sum",
        (struct((4 * hub_own, width), BF), struct((cols, 24, width), F32)),
        rows * depth * width,
        rows * depth * width * 2,
    )(first, bias_rows)
    second = swap(second, "col")

    third = call(
        col_sum_kernel,
        "col_sum",
        struct((rows, 32, width), BF),
        cols * 24 * width,
        cols * 24 * width * 4,
    )(second)
    third, grad_t, pg = lax.optimization_barrier((third, grad_t, pg))
    third = swap(third, "row")

    base = call(
        local_back_kernel,
        "local_back",
        struct((nodes, width), F32),
        2 * tiles * side * side * width + 2 * nodes * width * hidden,
        tiles * side * side * 2 + nodes * width * 10,
        in_specs=[HBM, HBM, HBM, VMEM, VMEM],
        scratch_shapes=[
            pltpu.SMEM((2, tiles), int32),
            pltpu.VMEM((width, hidden), BF),
            pltpu.VMEM((tile_steps, tile_block, side, side), BF),
            pltpu.VMEM((nodes // side, width, side), F32),
            sems(2 + tile_steps),
        ],
    )(tile_index, w_self, local_tiles, grad_t, pg)

    slot = jnp.arange(slots, dtype=jnp.int32)[None, :]
    listed = jnp.where(slot < send_counts[:, None], send_rows, -1)
    unused = jnp.full((1, slots - 3 * hub_own), -1, jnp.int32)
    hub_slots = jnp.concatenate([hub_rows, hub_rows, hub_rows, unused], axis=1)
    index = jnp.concatenate([listed, hub_slots], axis=0)
    index = jnp.pad(index, ((0, 16 - index.shape[0]), (0, 0)), constant_values=-1)
    grad_features = call(
        scatter_kernel,
        "scatter",
        struct((nodes, width), BF),
        2 * nodes * received_rows * width,
        nodes * width * 6 + received_rows * width * 2,
        grid=(steps,),
        in_specs=[
            whole((16, slots)),
            whole((4 * hub_own, width)),
            pl.BlockSpec((block, width), lambda i: (i, 0)),
        ]
        + [whole(part.shape) for part in returned],
        out_specs=pl.BlockSpec((block, width), lambda i: (i, 0)),
    )(index, hub_mine, base, *returned)

    factor = 1.0 / math.sqrt(nodes * rows * cols)

    def finish(*refs):
        finish_kernel(*refs, factor=factor)

    grad_self, grad_neigh, grad_bias = call(
        finish,
        "finish",
        (struct((width, hidden), F32), struct((width, hidden), F32), struct((1, hidden), F32)),
        rows * 24 * width,
        rows * 24 * width * 4,
    )(third)
    return grad_features, grad_self, grad_neigh, grad_bias.reshape(hidden)


def solution(mesh):
    placed = (
        P(("row", "col"), None),
        P(),
        P(),
        P(),
        P(("row", "col"), None),
        P(("row", "col"), None, None),
        P(("row", "col"), None),
        P(("row", "col"), None),
        P(("row", "col"), None),
        P(("row", "col")),
        P(("row", "col"), None),
        P(("row", "col"), None),
    )
    return jax.shard_map(
        body,
        mesh=mesh,
        in_specs=placed,
        out_specs=(P(("row", "col"), None), P(), P(), P()),
        check_vma=False,
    )
```
